32 devices in a mesh: train: 8 (over z, y), tile: 4 (over x, core).
Axes of the slice: x: 2, y: 2, z: 4, core: 2. Of those that a mesh axis runs over, the one named last changes fastest.
Arguments:
- test_grads: bfloat16 [1024, 4096], P('train', 'tile'), may hold values from -6 to 6
- fisher: bfloat16 [8, 512, 512], P('tile'), may hold values from -8 to 8
- train_grads: bfloat16 [32768, 4096], P(('train', 'tile')), may hold values from -0.09375 to 0.09375
- candidates: int32 [1024, 4], P('train'), may hold values from 0 to 7, all different within a row; in each aligned block of 128 rows (0 to 127, 128 to 255, ...) at most 96 rows name the same one
- shard_rows: int32 [8], P('train'), may hold values from 1024 to 4096
Outputs:
- top_scores: float32 [1024, 32], P('train')
The draws below stay inside these ranges and needn't reach their ends.
Inputs may be any that keep to these rules, and one draw needn't show every extreme that they name: `candidates`: each row names 4 different shards; among the rows of one index of train no shard is named by more than 96 rows.
All inputs are finite; a program needn't handle non-finite values.
Results may differ from the reference program's by a relative error of at most 0.0011.
Values may be sent and summed in bfloat16 or wider, within the bound.
A program may use at most 128 MiB of HBM per device.

```python
import math
import jax
import jax.numpy as jnp
import numpy as np
from jax import lax

K = 4096
BLOCK = 512
NB = 8
Q_DEV = 128
CANDS = 4
TOPK = 32
CAP = 96
SLOTS = 768
SHARD = 4096
TESTS = 1024
TRAIN_ROWS = 32768
N_TRAIN = 8


def draw_fisher(key, part):
    first_key, second_key = jax.random.split(key, 2)
    offdiag = jnp.clip(jax.random.normal(first_key, (NB, BLOCK, BLOCK), jnp.float32), -4.0, 4.0) * (0.6 / math.sqrt(BLOCK))
    diagonal = jnp.exp(jax.random.uniform(second_key, (NB, BLOCK), jnp.float32, math.log(0.5), math.log(2.0)))
    identity = jnp.arange(BLOCK)[:, None] == jnp.arange(BLOCK)[None, :]
    blocks = jnp.where(identity[None, :, :], diagonal[:, :, None], offdiag)
    return blocks.astype(jnp.bfloat16)


def set_ends(drawn, rng, low, high):
    shape = drawn.shape
    spot = [jax.random.randint(jax.random.fold_in(rng, axis), (), 0, shape[axis]) for axis in range(len(shape))]
    drawn = drawn.at[tuple(spot)].set(low)
    longest = shape.index(max(shape))
    spot[longest] = (spot[longest] + 1) % shape[longest]
    return drawn.at[tuple(spot)].set(high)


def levels(stream_key, shape, cuts, least, high):
    gain, own = 1.0, jax.random.fold_in(stream_key, 6)
    for axis_at, shards_of in cuts:
        draws = jnp.exp(jax.random.uniform(jax.random.fold_in(own, axis_at), (shards_of,), jnp.float32, least / len(cuts), high / len(cuts)))
        gain = gain * jnp.repeat(draws, shape[axis_at] // shards_of).reshape([-1 if axis == axis_at else 1 for axis in range(len(shape))])
    return gain


def shared_out(stream_key, own, number, rows, count, top, bound, slope):
    order = jax.random.permutation(stream_key, count)
    crowded, ordinary = load_shares(count, rows * top, bound, slope, True), load_shares(count, rows * top, bound, slope, False)
    places = jnp.arange(count)

    def named(sizes, rotation):
        used = int((sizes > 0).sum())
        fixed = max(1, used // 4)
        passed = fixed + (places - fixed + rotation * (used - fixed)) % max(1, count - fixed)
        return jnp.zeros((count,), jnp.int32).at[order[jnp.where(places < fixed, places, passed)]].set(jnp.asarray(sizes, jnp.int32))

    sizes = jnp.where(number % 4 == 0, named(crowded, number // 4), named(ordinary, number - number // 4 - 1))
    mixed = jax.random.permutation(jax.random.fold_in(own, 3), count)
    donor, taker = mixed[0:count // 2 * 2:2], mixed[1:count // 2 * 2:2]
    slack = jnp.minimum(sizes[donor] - 1, bound - sizes[taker]) // 2
    slack = jnp.where((donor == order[0]) | (taker == order[0]) | (sizes[taker] == 0), 0, jnp.maximum(slack, 0))
    passed = jax.random.randint(jax.random.fold_in(own, 4), (count // 2,), 0, 1 << 20) % (slack + 1)
    sizes = sizes.at[donor].add(-passed).at[taker].add(passed)
    labels = jnp.searchsorted(jnp.cumsum(sizes), jnp.arange(rows * top), side="right").astype(jnp.int32)
    grid = labels.reshape(top, rows).T
    grid = grid[jax.random.permutation(jax.random.fold_in(own, 1), rows)]
    rotation = jax.random.randint(jax.random.fold_in(own, 2), (rows, 1), 0, top)
    return jnp.take_along_axis(grid, (jnp.arange(top)[None, :] + rotation) % top, axis=1)


def load_shares(amount, total, reach, skew, full):
    loads = [(1 << 20) // math.isqrt(grade ** skew) + 1 for grade in range(1, amount + 1)]
    largest = reach if full else min(reach, max(-(-total // amount), total * loads[0] // sum(loads)))
    least = 1 if total - largest >= amount - 1 else 0
    counts, surplus = [largest] + [least] * (amount - 1), total - largest - least * (amount - 1)
    while surplus > 0:
        free = [i for i in range(1, amount) if counts[i] < largest] or [i for i in range(1, amount) if counts[i] < reach]
        pool, remaining = sum([loads[i] for i in free]), surplus
        for i in free:
            more = min(reach - counts[i], max(1, remaining * loads[i] // pool), surplus)
            counts[i] = counts[i] + more
            surplus = surplus - more
    return np.array(counts)


def noise(own_key, dims, scale, limit, shards=(), held_as=jnp.bfloat16):
    result = scale * jax.random.normal(own_key, dims, jnp.float32)
    if shards:
        result = result * levels(own_key, dims, shards, -0.22, 0.18)
    return jnp.clip(result, -limit, limit).astype(held_as)


def setup_inputs(seed: int = 0) -> dict:
    key_list = jax.random.split(jax.random.key(seed), 6)
    test_grads = noise(key_list[0], (TESTS, K), 1.0, 6.0, ((0, 8), (1, 4)))
    fisher = draw_fisher(jax.random.fold_in(key_list[5], 71), 0)
    train_grads = noise(key_list[2], (TRAIN_ROWS, K), K ** -0.5, 0.09375, ((0, 32),))
    candidates_keys = jax.random.split(jax.random.fold_in(key_list[3], 1), TESTS // Q_DEV)
    candidates_turns = jax.random.permutation(jax.random.fold_in(key_list[3], 3), TESTS // Q_DEV)
    candidates = jax.vmap(lambda own, number: shared_out(jax.random.fold_in(key_list[3], 2), own, number, Q_DEV, N_TRAIN, CANDS, CAP, 2))(candidates_keys, candidates_turns).reshape((TESTS, CANDS))
    shard_rows = set_ends(jax.random.randint(key_list[4], (N_TRAIN,), SHARD // 4, SHARD + 1), jax.random.fold_in(key_list[4], 1), SHARD // 4, SHARD).astype(jnp.int32)
    return dict(test_grads=test_grads, fisher=fisher, train_grads=train_grads, candidates=candidates, shard_rows=shard_rows)


lowest_score = -1.0e30


def reference(test_grads, fisher, train_grads, candidates, shard_rows):
    test_count = test_grads.shape[0]
    blocks = fisher.shape[0]
    block_order = fisher.shape[1]
    precond = jnp.einsum("qbi,bij->qbj", test_grads.astype(jnp.float32).reshape(test_count, blocks, block_order), fisher.astype(jnp.float32))
    precond = precond.reshape(test_count, blocks * block_order).astype(jnp.bfloat16)
    padded = jnp.concatenate([precond.astype(jnp.float32), jnp.zeros((1, blocks * block_order), jnp.float32)], axis=0)
    shard_grads = train_grads.reshape(N_TRAIN, SHARD, K)

    def advance(leaders, inputs):
        shard_block, shard_id = inputs
        naming = jnp.any(candidates == shard_id, axis=1)
        picked = jnp.nonzero(naming, size=SLOTS, fill_value=test_count)[0].astype(jnp.int32)
        scores = jnp.dot(padded[picked], shard_block.astype(jnp.float32).T)
        alive_rows = jnp.arange(SHARD, dtype=jnp.int32) < shard_rows[shard_id]
        scores = jnp.where(alive_rows[None, :], scores, lowest_score)
        highest = lax.top_k(scores, TOPK)[0]
        merged = lax.top_k(jnp.concatenate([leaders[picked], highest], axis=1), TOPK)[0]
        return leaders.at[picked].set(merged), None

    initial = jnp.full((test_count + 1, TOPK), lowest_score, jnp.float32)
    leaders, _ = lax.scan(advance, initial, (shard_grads, jnp.arange(N_TRAIN, dtype=jnp.int32)))
    return leaders[:test_count]
```

```python
import functools

import jax
import jax.numpy as jnp
from jax import lax
from jax.experimental import pallas as pl
from jax.experimental.pallas import tpu as pltpu
from jax.sharding import PartitionSpec as P

TOPK = 32
MESH = pl.DeviceIdType.MESH

lowest_score = -1e30


def combined_all(part, axis, combine):
    gathered = lax.all_gather(part, axis)

    def take(source):
        return lax.dynamic_index_in_dim(gathered, source, 0, False)

    return lax.fori_loop(
        1, lax.axis_size(axis), lambda source, state: combine(state, take(source)), take(0)
    )


def combine_leaders(earlier_best, later_best):
    joined = jnp.concatenate([earlier_best, later_best], axis=-1)
    return lax.top_k(joined, earlier_best.shape[-1])[0]


def shards(test_grads, fisher, train_grads, candidates, shard_rows):
    train_count = lax.axis_size("train")
    q_rows, columns = test_grads.shape
    blocks, block_order, _ = fisher.shape
    cand_count = candidates.shape[1]
    local_rows = train_grads.shape[0]
    capacity = max(2, 3 * q_rows * cand_count // (2 * train_count))
    precond = jnp.einsum(
        "qbi,bij->qbj",
        test_grads.reshape(q_rows, blocks, block_order),
        fisher,
        preferred_element_type=jnp.float32,
    )
    precond = precond.reshape(q_rows, columns).astype(jnp.bfloat16)
    targets = candidates.reshape(-1)
    one_hot = (targets[:, None] == jnp.arange(train_count, dtype=jnp.int32)[None, :]).astype(
        jnp.int32
    )
    earlier = jnp.cumsum(one_hot, axis=0) - one_hot
    rank_in = jnp.sum(earlier * one_hot, axis=1)
    slot_index = targets * capacity + rank_in
    sources = jnp.arange(q_rows * cand_count, dtype=jnp.int32) // cand_count
    owner_row = jnp.full((train_count * capacity,), q_rows, jnp.int32).at[slot_index].set(sources)
    row_ids = lax.axis_index("tile") * local_rows + jnp.arange(local_rows, dtype=jnp.int32)
    alive_rows = row_ids < shard_rows[0]
    complete = lax.all_gather(precond, "tile", axis=1, tiled=True)
    padded = jnp.concatenate([complete, jnp.zeros((1, complete.shape[1]), jnp.bfloat16)], axis=0)
    outgoing = padded[owner_row].reshape(train_count, capacity, complete.shape[1])
    scores = jnp.einsum(
        "nck,rk->ncr",
        lax.all_to_all(outgoing, "train", split_axis=0, concat_axis=0, tiled=True),
        train_grads,
        preferred_element_type=jnp.float32,
    )
    masked = jnp.where(alive_rows, scores, lowest_score)
    leaders = lax.top_k(masked, TOPK)[0]
    leaders = combined_all(leaders, "tile", combine_leaders)
    returned = lax.all_to_all(leaders, "train", split_axis=0, concat_axis=0, tiled=True)
    flattened = returned.reshape(train_count * capacity, TOPK)
    per_pair = flattened[slot_index].reshape(q_rows, cand_count * TOPK)
    result_best = lax.top_k(per_pair, TOPK)[0]
    return result_best


def batcher(n):
    pairs = []
    p = 1
    while p < n:
        k = p
        while k >= 1:
            for j in range(k % p, n - k, 2 * k):
                for i in range(min(k, n - j - k)):
                    if (i + j) // (2 * p) == (i + j + k) // (2 * p):
                        pairs.append((i + j, i + j + k))
            k //= 2
        p *= 2
    return pairs


def sort_down(values):
    values = list(values)
    for i, j in batcher(len(values)):
        a, b = values[i], values[j]
        values[i], values[j] = jnp.maximum(a, b), jnp.minimum(a, b)
    return values


def merge_top(first, second):
    n = len(first)
    values = [jnp.maximum(first[i], second[n - 1 - i]) for i in range(n)]
    d = n // 2
    while d >= 1:
        for i in range(n):
            if not i & d:
                a, b = values[i], values[i + d]
                values[i], values[i + d] = jnp.maximum(a, b), jnp.minimum(a, b)
        d //= 2
    return values


def over_sublanes(values):
    for shift in (4, 2, 1):
        values = merge_top(values, [pltpu.roll(v, shift, 0) for v in values])
    return values


def kernel(
    test_ref, fisher_ref, train_hbm, cand_ref, rows_ref, out_ref,
    train, gathered, acc, best, sent, homed, tiles, send_sem, recv_sem, load_sem,
):
    me, tile = lax.axis_index("train"), lax.axis_index("tile")
    z, y = me // 2, me % 2
    x, core = tile // 2, tile % 2
    q = test_ref.shape[0]
    half = q // 2
    width = test_ref.shape[1]
    order = fisher_ref.shape[1]
    local_rows = train.shape[0]

    zs = [z, z + 1 - 2 * (z % 2), (z + 2) % 4, 3 - z]
    ys = [y, 1 - y]
    at_tile = [tile, x * 2 + 1 - core, (1 - x) * 2 + core, (1 - x) * 2 + 1 - core]

    def home(k, yr):
        return (zs[k] * 2 + ys[yr], tile)

    def at(t):
        return (me, at_tile[t])

    load = pltpu.make_async_copy(train_hbm, train, load_sem)
    load.start()
    barrier = pltpu.get_barrier_semaphore()
    peers = [home(k, yr) for k in range(4) for yr in range(2) if k or yr]
    peers += [at(t) for t in range(1, 4)]
    for peer in peers:
        pl.semaphore_signal(barrier, inc=1, device_id=peer, device_id_type=MESH)

    for b in range(fisher_ref.shape[0]):
        columns = slice(b * order, (b + 1) * order)
        gathered[0, 0, :q, columns] = jnp.dot(
            test_ref[:, columns], fisher_ref[b], preferred_element_type=jnp.float32
        ).astype(jnp.bfloat16)
    homed[...] = jnp.full_like(homed, lowest_score)
    tiles[...] = jnp.full_like(tiles, lowest_score)
    pl.semaphore_wait(barrier, len(peers))

    copies = {}

    def send(name, source, target, device):
        n = len(copies)
        copies[name] = pltpu.make_async_remote_copy(
            src_ref=source, dst_ref=target, send_sem=send_sem.at[n], recv_sem=recv_sem.at[n],
            device_id=device, device_id_type=MESH,
        )
        copies[name].start()

    def rows(k, t, start, count):
        return gathered.at[k, t, pl.ds(start, count)]

    def over_z(k):
        send(("z", k), rows(0, 0, 0, q), rows(k, 0, 0, q), home(k, 0))

    def first(k):
        send(("y", k), rows(k, 0, 0, q), rows(k, 0, q, q), home(0, 1))
        send(("x", k), rows(k, 0, 0, q), rows(k, 2, 0, q), at(2))
        send(("s00", k), rows(k, 0, 0, q), rows(k, 1, 0, q), at(1))

    def second(k):
        copies["y", k].wait_recv()
        send(("x2", k), rows(k, 0, q, half), rows(k, 2, q, half), at(2))
        copies["x", k].wait_recv()
        send(("y2", k), rows(k, 2, half, half), rows(k, 2, q + half, half), home(0, 1))
        send(("s10", k), rows(k, 0, q, q), rows(k, 1, q, q), at(1))
        send(("s01", k), rows(k, 2, 0, q), rows(k, 3, 0, q), at(1))

    def third(k):
        copies["x2", k].wait_recv()
        copies["y2", k].wait_recv()
        send(("s11", k), rows(k, 2, q, q), rows(k, 3, q, q), at(1))
        for name in ("s00", "s10", "s01", "s11"):
            copies[name, k].wait_recv()

    def compute(k):
        def multiply(t, carry):
            xr, cr = t // 2, t % 2
            xt = x + xr - 2 * x * xr
            ct = core + cr - 2 * core * cr
            start = pl.multiple_of((xt * 2 + ct) * width, width)
            part = lax.dot_general(
                train[:, pl.ds(start, width)], gathered[k, t],
                (((1,), (1,)), ((), ())), preferred_element_type=jnp.float32,
            )
            for g in range(2):
                acc[g] += part[:, g * q:(g + 1) * q]
            return carry

        acc[...] = jnp.zeros_like(acc)
        lax.fori_loop(0, 4, multiply, 0)

        live = rows_ref[0] - tile * local_rows
        step = 8 * TOPK

        def lanes(g, carry):
            best[...] = jnp.full_like(best, lowest_score)

            def block(j, carry):
                base = pl.multiple_of(j * step, step)
                ids = lax.broadcasted_iota(jnp.int32, (8, q), 0) + base
                values = []
                for i in range(TOPK):
                    value = acc[g, pl.ds(base + 8 * i, 8), :]
                    values.append(jnp.where(ids + 8 * i < live, value, lowest_score))
                merged = merge_top([best[i] for i in range(TOPK)], sort_down(values))
                for i in range(TOPK):
                    best[i] = merged[i]
                return carry

            lax.fori_loop(0, local_rows // step, block, 0)
            merged = over_sublanes([best[i] for i in range(TOPK)])
            for i in range(TOPK):
                sent[k, g, i:i + 1, :] = merged[i][0:1]
            return carry

        lax.fori_loop(0, 2, lanes, 0)
        for yr in range(2):
            slot = k * 2 + yr
            if slot:
                send(("h", slot), sent.at[k, yr], homed.at[pl.ds(slot * TOPK, TOPK)], home(k, yr))
            else:
                homed[0:TOPK] = sent[0, 0]

    over_z(1)
    over_z(2)
    first(0)
    copies["z", 1].wait_recv()
    first(1)
    second(0)
    copies["z", 2].wait_recv()
    over_z(3)
    first(2)
    third(0)
    load.wait()
    compute(0)
    second(1)
    copies["z", 3].wait_recv()
    first(3)
    third(1)
    compute(1)
    second(2)
    third(2)
    second(3)
    compute(2)
    third(3)
    compute(3)

    for slot in range(1, 8):
        copies["h", slot].wait_recv()
    slots = lax.broadcasted_iota(jnp.int32, (8, q), 0)
    kv, yv = slots // 2, slots % 2
    shard = jnp.zeros_like(slots)
    for k in range(4):
        shard = jnp.where(kv == k, zs[k] * 2, shard)
    shard = shard + jnp.where(yv == 0, ys[0], ys[1])
    named = shard == cand_ref[0:1, :]
    for c in range(1, cand_ref.shape[0]):
        named = named | (shard == cand_ref[c:c + 1, :])
    merged = over_sublanes([
        jnp.where(named, homed[pl.ds(i, 8, stride=TOPK), :], lowest_score) for i in range(TOPK)
    ])
    for i in range(TOPK):
        tiles[i:i + 1, :] = merged[i][0:1]
    for t in range(1, 4):
        send(("t", t), tiles.at[pl.ds(0, TOPK)], tiles.at[pl.ds(t * TOPK, TOPK)], at(t))
    for t in range(1, 4):
        copies["t", t].wait_recv()
    merged = over_sublanes([tiles[pl.ds(i, 8, stride=TOPK), :] for i in range(TOPK)])
    for i in range(TOPK):
        out_ref[i:i + 1, :] = merged[i][0:1]
    for copy in copies.values():
        copy.wait_send()


def fused(test_grads, fisher, train_grads, candidates, shard_rows):
    q, width = test_grads.shape
    local_rows, columns = train_grads.shape
    vmem = pl.BlockSpec(memory_space=pltpu.VMEM)
    best = pl.pallas_call(
        kernel,
        out_shape=jax.ShapeDtypeStruct((TOPK, q), jnp.float32),
        in_specs=[
            vmem, vmem, pl.BlockSpec(memory_space=pl.ANY), vmem,
            pl.BlockSpec(memory_space=pltpu.SMEM),
        ],
        out_specs=vmem,
        scratch_shapes=[
            pltpu.VMEM((local_rows, columns), jnp.bfloat16),
            pltpu.VMEM((4, 4, 2 * q, width), jnp.bfloat16),
            pltpu.VMEM((2, local_rows, q), jnp.float32),
            pltpu.VMEM((TOPK, 8, q), jnp.float32),
            pltpu.VMEM((4, 2, TOPK, q), jnp.float32),
            pltpu.VMEM((8 * TOPK, q), jnp.float32),
            pltpu.VMEM((8 * TOPK, q), jnp.float32),
            pltpu.SemaphoreType.DMA((48,)),
            pltpu.SemaphoreType.DMA((48,)),
            pltpu.SemaphoreType.DMA,
        ],
        compiler_params=pltpu.CompilerParams(
            collective_id=0, has_side_effects=True, vmem_limit_bytes=40 * 1024 * 1024
        ),
    )(test_grads, fisher, train_grads, candidates.T, shard_rows)
    return best.T


def solution(mesh):
    placed = (
        P("train", "tile"),
        P("tile", None, None),
        P(("train", "tile"), None),
        P("train", None),
        P("train"),
    )
    sizes = (mesh.shape["train"], mesh.shape["tile"])
    return jax.shard_map(
        fused if sizes == (8, 4) else shards,
        mesh=mesh, in_specs=placed, out_specs=P("train", None), check_vma=False,
    )
```

```python
import functools

import jax
import jax.numpy as jnp
from jax import lax
from jax.experimental import pallas as pl
from jax.experimental.pallas import tpu as pltpu
from jax.sharding import PartitionSpec as P

TOPK = 32
MESH = pl.DeviceIdType.MESH

lowest_score = -1e30


def combined_all(part, axis, combine):
    gathered = lax.all_gather(part, axis)

    def take(source):
        return lax.dynamic_index_in_dim(gathered, source, 0, False)

    return lax.fori_loop(
        1, lax.axis_size(axis), lambda source, state: combine(state, take(source)), take(0)
    )


def combine_leaders(earlier_best, later_best):
    joined = jnp.concatenate([earlier_best, later_best], axis=-1)
    return lax.top_k(joined, earlier_best.shape[-1])[0]


def shards(test_grads, fisher, train_grads, candidates, shard_rows):
    train_count = lax.axis_size("train")
    q_rows, columns = test_grads.shape
    blocks, block_order, _ = fisher.shape
    cand_count = candidates.shape[1]
    local_rows = train_grads.shape[0]
    capacity = max(2, 3 * q_rows * cand_count // (2 * train_count))
    precond = jnp.einsum(
        "qbi,bij->qbj",
        test_grads.reshape(q_rows, blocks, block_order),
        fisher,
        preferred_element_type=jnp.float32,
    )
    precond = precond.reshape(q_rows, columns).astype(jnp.bfloat16)
    targets = candidates.reshape(-1)
    one_hot = (targets[:, None] == jnp.arange(train_count, dtype=jnp.int32)[None, :]).astype(
        jnp.int32
    )
    earlier = jnp.cumsum(one_hot, axis=0) - one_hot
    rank_in = jnp.sum(earlier * one_hot, axis=1)
    slot_index = targets * capacity + rank_in
    sources = jnp.arange(q_rows * cand_count, dtype=jnp.int32) // cand_count
    owner_row = jnp.full((train_count * capacity,), q_rows, jnp.int32).at[slot_index].set(sources)
    row_ids = lax.axis_index("tile") * local_rows + jnp.arange(local_rows, dtype=jnp.int32)
    alive_rows = row_ids < shard_rows[0]
    complete = lax.all_gather(precond, "tile", axis=1, tiled=True)
    padded = jnp.concatenate([complete, jnp.zeros((1, complete.shape[1]), jnp.bfloat16)], axis=0)
    outgoing = padded[owner_row].reshape(train_count, capacity, complete.shape[1])
    scores = jnp.einsum(
        "nck,rk->ncr",
        lax.all_to_all(outgoing, "train", split_axis=0, concat_axis=0, tiled=True),
        train_grads,
        preferred_element_type=jnp.float32,
    )
    masked = jnp.where(alive_rows, scores, lowest_score)
    leaders = lax.top_k(masked, TOPK)[0]
    leaders = combined_all(leaders, "tile", combine_leaders)
    returned = lax.all_to_all(leaders, "train", split_axis=0, concat_axis=0, tiled=True)
    flattened = returned.reshape(train_count * capacity, TOPK)
    per_pair = flattened[slot_index].reshape(q_rows, cand_count * TOPK)
    result_best = lax.top_k(per_pair, TOPK)[0]
    return result_best


def batcher(n):
    pairs = []
    p = 1
    while p < n:
        k = p
        while k >= 1:
            for j in range(k % p, n - k, 2 * k):
                for i in range(min(k, n - j - k)):
                    if (i + j) // (2 * p) == (i + j + k) // (2 * p):
                        pairs.append((i + j, i + j + k))
            k //= 2
        p *= 2
    return pairs


def sort_down(values):
    values = list(values)
    for i, j in batcher(len(values)):
        a, b = values[i], values[j]
        values[i], values[j] = jnp.maximum(a, b), jnp.minimum(a, b)
    return values


def merge_top(first, second):
    n = len(first)
    values = [jnp.maximum(first[i], second[n - 1 - i]) for i in range(n)]
    d = n // 2
    while d >= 1:
        for i in range(n):
            if not i & d:
                a, b = values[i], values[i + d]
                values[i], values[i + d] = jnp.maximum(a, b), jnp.minimum(a, b)
        d //= 2
    return values


def over_sublanes(values):
    for shift in (4, 2, 1):
        values = merge_top(values, [pltpu.roll(v, shift, 0) for v in values])
    return values


def kernel(
    test_hbm, fisher_hbm, train_hbm, cand_hbm, rows_ref, out_ref,
    test, fisher, train, cand, gathered, acc, best, sent, homed, tiles,
    send_sem, recv_sem, load_sem,
):
    me, tile = lax.axis_index("train"), lax.axis_index("tile")
    z, y = me // 2, me % 2
    x, core = tile // 2, tile % 2
    q, width = test.shape
    half = q // 2
    order = fisher.shape[1]
    local_rows = train.shape[0]

    inner = (z == 1) | (z == 2)
    outer = (z == 0) | (z == 3)
    flag = ((z + 1) // 2) % 2
    across, two_on = 3 - z, (z + 2) % 4
    zs = [
        z,
        z + 1 - 2 * (z % 2),
        two_on + flag * (across - two_on),
        across + flag * (two_on - across),
    ]
    ys = [y, 1 - y]
    at_tile = [tile, x * 2 + 1 - core, (1 - x) * 2 + core, (1 - x) * 2 + 1 - core]

    def home(a, yr):
        return (zs[a] * 2 + ys[yr], tile)

    def at(t):
        return (me, at_tile[t])

    loads = [
        pltpu.make_async_copy(test_hbm, test, load_sem.at[0]),
        pltpu.make_async_copy(fisher_hbm, fisher, load_sem.at[1]),
        pltpu.make_async_copy(cand_hbm, cand, load_sem.at[2]),
    ]
    for t in range(4):
        start = pl.multiple_of(at_tile[t] * width, width)
        loads.append(pltpu.make_async_copy(
            train_hbm.at[:, pl.ds(start, width)],
            train.at[:, pl.ds(t * width, width)],
            load_sem.at[3 + t],
        ))
    for load in loads:
        load.start()
    barrier = pltpu.get_barrier_semaphore()
    peers = [home(a, yr) for a in range(4) for yr in range(2) if a or yr]
    peers += [at(t) for t in range(1, 4)]
    for peer in peers:
        pl.semaphore_signal(barrier, inc=1, device_id=peer, device_id_type=MESH)

    homed[...] = jnp.full_like(homed, lowest_score)
    tiles[...] = jnp.full_like(tiles, lowest_score)
    loads[0].wait()
    loads[1].wait()
    for b in range(fisher.shape[0]):
        columns = slice(b * order, (b + 1) * order)
        gathered[0, :q, columns] = jnp.dot(
            test[:, columns], fisher[b], preferred_element_type=jnp.float32
        ).astype(jnp.bfloat16)
    pl.semaphore_wait(barrier, len(peers))

    copies = {}

    def copy_to(n, got, source, target, device):
        return pltpu.make_async_remote_copy(
            src_ref=source, dst_ref=target, send_sem=send_sem.at[n], recv_sem=recv_sem.at[got],
            device_id=device, device_id_type=MESH,
        )

    def send(name, source, target, device):
        n = len(copies) + 8
        copies[name] = copy_to(n, n, source, target, device)
        copies[name].start()

    def rows(a, t, start, count):
        return gathered.at[a, pl.ds(start, count), pl.ds(t * width, width)]

    def unit(a):
        return rows(a, 0, 0, q)

    to_pair = copy_to(0, 1, unit(0), unit(1), home(1, 0))
    inner_copies = [
        copy_to(1, 2, unit(0), unit(2), (across * 2 + y, tile)),
        copy_to(2, 3, unit(1), unit(3), (across * 2 + y, tile)),
        copy_to(3, 2, unit(2), unit(2), home(1, 0)),
        copy_to(4, 3, unit(3), unit(3), home(1, 0)),
    ]

    def arrived(a):
        copy_to(0, a, unit(0), unit(a), home(1, 0)).wait_recv()

    def first(a):
        send(("y", a), rows(a, 0, 0, q), rows(a, 0, q, q), home(0, 1))
        send(("x", a), rows(a, 0, 0, q), rows(a, 2, 0, q), at(2))
        send(("s00", a), rows(a, 0, 0, q), rows(a, 1, 0, q), at(1))

    def second(a):
        copies["y", a].wait_recv()
        send(("x2", a), rows(a, 0, q, half), rows(a, 2, q, half), at(2))
        copies["x", a].wait_recv()
        send(("y2", a), rows(a, 2, half, half), rows(a, 2, q + half, half), home(0, 1))
        send(("s10", a), rows(a, 0, q, q), rows(a, 1, q, q), at(1))
        send(("s01", a), rows(a, 2, 0, q), rows(a, 3, 0, q), at(1))

    def third(a):
        copies["x2", a].wait_recv()
        copies["y2", a].wait_recv()
        send(("s11", a), rows(a, 2, q, q), rows(a, 3, q, q), at(1))
        for name in ("s00", "s10", "s01", "s11"):
            copies[name, a].wait_recv()

    def compute(a):
        part_rows = local_rows // 2

        def multiply(r, carry):
            start = pl.multiple_of(r * part_rows, part_rows)
            part = lax.dot_general(
                train[pl.ds(start, part_rows), :], gathered[a],
                (((1,), (1,)), ((), ())), preferred_element_type=jnp.float32,
            )
            for g in range(2):
                acc[g, pl.ds(start, part_rows), :] = part[:, g * q:(g + 1) * q]
            return carry

        lax.fori_loop(0, 2, multiply, 0)

        live = rows_ref[0] - tile * local_rows
        step = 8 * TOPK

        def lanes(g, carry):
            best[...] = jnp.full_like(best, lowest_score)

            def block(j, carry):
                base = pl.multiple_of(j * step, step)
                ids = lax.broadcasted_iota(jnp.int32, (8, q), 0) + base
                values = []
                for i in range(TOPK):
                    value = acc[g, pl.ds(base + 8 * i, 8), :]
                    values.append(jnp.where(ids + 8 * i < live, value, lowest_score))
                merged = merge_top([best[i] for i in range(TOPK)], sort_down(values))
                for i in range(TOPK):
                    best[i] = merged[i]
                return carry

            lax.fori_loop(0, local_rows // step, block, 0)
            merged = over_sublanes([best[i] for i in range(TOPK)])
            for i in range(TOPK):
                sent[a, g, i:i + 1, :] = merged[i][0:1]
            return carry

        lax.fori_loop(0, 2, lanes, 0)
        for yr in range(2):
            if a or yr:
                n = len(copies) + 8
                copies["h", a, yr] = copy_to(
                    n, 52 + me, sent.at[a, yr], homed.at[pl.ds(me * TOPK, TOPK)], home(a, yr)
                )
                copies["h", a, yr].start()
            else:
                homed[pl.ds(pl.multiple_of(me * TOPK, TOPK), TOPK)] = sent[0, 0]

    to_pair.start()

    @pl.when(inner)
    def _():
        inner_copies[0].start()

    first(0)
    arrived(1)

    @pl.when(inner)
    def _():
        inner_copies[1].start()
        arrived(2)
        inner_copies[2].start()

    first(1)
    second(0)

    @pl.when(inner)
    def _():
        arrived(3)
        inner_copies[3].start()

    @pl.when(outer)
    def _():
        arrived(2)

    first(2)
    third(0)
    for load in loads[2:]:
        load.wait()
    compute(0)
    second(1)

    @pl.when(outer)
    def _():
        arrived(3)

    first(3)
    third(1)
    compute(1)
    second(2)
    second(3)
    third(2)
    compute(2)
    third(3)
    compute(3)

    for d in range(1, 8):
        source = (me + d) % 8
        copy_to(
            0, 52 + source, sent.at[0, 0], homed.at[pl.ds(source * TOPK, TOPK)], home(0, 1)
        ).wait_recv()
    shard = lax.broadcasted_iota(jnp.int32, (8, q), 0)
    named = shard == cand[0:1, :]
    for c in range(1, cand.shape[0]):
        named = named | (shard == cand[c:c + 1, :])
    merged = over_sublanes([
        jnp.where(named, homed[pl.ds(i, 8, stride=TOPK), :], lowest_score) for i in range(TOPK)
    ])
    for i in range(TOPK):
        tiles[i:i + 1, :] = merged[i][0:1]
    for t in range(1, 4):
        send(("t", t), tiles.at[pl.ds(0, TOPK)], tiles.at[pl.ds(t * TOPK, TOPK)], at(t))
    for t in range(1, 4):
        copies["t", t].wait_recv()
    merged = over_sublanes([tiles[pl.ds(i, 8, stride=TOPK), :] for i in range(TOPK)])
    for i in range(TOPK):
        out_ref[i:i + 1, :] = merged[i][0:1]
    for copy in copies.values():
        copy.wait_send()
    to_pair.wait_send()

    @pl.when(inner)
    def _():
        for copy in inner_copies:
            copy.wait_send()


def fused(test_grads, fisher, train_grads, candidates, shard_rows):
    q, width = test_grads.shape
    local_rows, columns = train_grads.shape
    anywhere = pl.BlockSpec(memory_space=pl.ANY)
    best = pl.pallas_call(
        kernel,
        out_shape=jax.ShapeDtypeStruct((TOPK, q), jnp.float32),
        in_specs=[anywhere] * 4 + [pl.BlockSpec(memory_space=pltpu.SMEM)],
        out_specs=pl.BlockSpec(memory_space=pltpu.VMEM),
        scratch_shapes=[
            pltpu.VMEM(test_grads.shape, jnp.bfloat16),
            pltpu.VMEM(fisher.shape, jnp.bfloat16),
            pltpu.VMEM((local_rows, columns), jnp.bfloat16),
            pltpu.VMEM(candidates.shape[::-1], jnp.int32),
            pltpu.VMEM((4, 2 * q, columns), jnp.bfloat16),
            pltpu.VMEM((2, local_rows, q), jnp.float32),
            pltpu.VMEM((TOPK, 8, q), jnp.float32),
            pltpu.VMEM((4, 2, TOPK, q), jnp.float32),
            pltpu.VMEM((8 * TOPK, q), jnp.float32),
            pltpu.VMEM((8 * TOPK, q), jnp.float32),
            pltpu.SemaphoreType.DMA((60,)),
            pltpu.SemaphoreType.DMA((60,)),
            pltpu.SemaphoreType.DMA((7,)),
        ],
        compiler_params=pltpu.CompilerParams(
            collective_id=0, has_side_effects=True, vmem_limit_bytes=56 * 1024 * 1024
        ),
    )(test_grads, fisher, train_grads, candidates.T, shard_rows)
    return best.T


def solution(mesh):
    placed = (
        P("train", "tile"),
        P("tile", None, None),
        P(("train", "tile"), None),
        P("train", None),
        P("train"),
    )
    sizes = (mesh.shape["train"], mesh.shape["tile"])
    return jax.shard_map(
        fused if sizes == (8, 4) else shards,
        mesh=mesh, in_specs=placed, out_specs=P("train", None), check_vma=False,
    )
```

```python
import functools

import jax
import jax.numpy as jnp
from jax import lax
from jax.experimental import pallas as pl
from jax.experimental.pallas import tpu as pltpu
from jax.sharding import PartitionSpec as P

TOPK = 32
MESH = pl.DeviceIdType.MESH

lowest_score = -1e30


def combined_all(part, axis, combine):
    gathered = lax.all_gather(part, axis)

    def take(source):
        return lax.dynamic_index_in_dim(gathered, source, 0, False)

    return lax.fori_loop(
        1, lax.axis_size(axis), lambda source, state: combine(state, take(source)), take(0)
    )


def combine_leaders(earlier_best, later_best):
    joined = jnp.concatenate([earlier_best, later_best], axis=-1)
    return lax.top_k(joined, earlier_best.shape[-1])[0]


def shards(test_grads, fisher, train_grads, candidates, shard_rows):
    train_count = lax.axis_size("train")
    q_rows, columns = test_grads.shape
    blocks, block_order, _ = fisher.shape
    cand_count = candidates.shape[1]
    local_rows = train_grads.shape[0]
    capacity = max(2, 3 * q_rows * cand_count // (2 * train_count))
    precond = jnp.einsum(
        "qbi,bij->qbj",
        test_grads.reshape(q_rows, blocks, block_order),
        fisher,
        preferred_element_type=jnp.float32,
    )
    precond = precond.reshape(q_rows, columns).astype(jnp.bfloat16)
    targets = candidates.reshape(-1)
    one_hot = (targets[:, None] == jnp.arange(train_count, dtype=jnp.int32)[None, :]).astype(
        jnp.int32
    )
    earlier = jnp.cumsum(one_hot, axis=0) - one_hot
    rank_in = jnp.sum(earlier * one_hot, axis=1)
    slot_index = targets * capacity + rank_in
    sources = jnp.arange(q_rows * cand_count, dtype=jnp.int32) // cand_count
    owner_row = jnp.full((train_count * capacity,), q_rows, jnp.int32).at[slot_index].set(sources)
    row_ids = lax.axis_index("tile") * local_rows + jnp.arange(local_rows, dtype=jnp.int32)
    alive_rows = row_ids < shard_rows[0]
    complete = lax.all_gather(precond, "tile", axis=1, tiled=True)
    padded = jnp.concatenate([complete, jnp.zeros((1, complete.shape[1]), jnp.bfloat16)], axis=0)
    outgoing = padded[owner_row].reshape(train_count, capacity, complete.shape[1])
    scores = jnp.einsum(
        "nck,rk->ncr",
        lax.all_to_all(outgoing, "train", split_axis=0, concat_axis=0, tiled=True),
        train_grads,
        preferred_element_type=jnp.float32,
    )
    masked = jnp.where(alive_rows, scores, lowest_score)
    leaders = lax.top_k(masked, TOPK)[0]
    leaders = combined_all(leaders, "tile", combine_leaders)
    returned = lax.all_to_all(leaders, "train", split_axis=0, concat_axis=0, tiled=True)
    flattened = returned.reshape(train_count * capacity, TOPK)
    per_pair = flattened[slot_index].reshape(q_rows, cand_count * TOPK)
    result_best = lax.top_k(per_pair, TOPK)[0]
    return result_best


def batcher(n):
    pairs = []
    p = 1
    while p < n:
        k = p
        while k >= 1:
            for j in range(k % p, n - k, 2 * k):
                for i in range(min(k, n - j - k)):
                    if (i + j) // (2 * p) == (i + j + k) // (2 * p):
                        pairs.append((i + j, i + j + k))
            k //= 2
        p *= 2
    return pairs


def sort_down(values):
    values = list(values)
    for i, j in batcher(len(values)):
        a, b = values[i], values[j]
        values[i], values[j] = jnp.maximum(a, b), jnp.minimum(a, b)
    return values


def merge_top(first, second):
    n = len(first)
    values = [jnp.maximum(first[i], second[n - 1 - i]) for i in range(n)]
    d = n // 2
    while d >= 1:
        for i in range(n):
            if not i & d:
                a, b = values[i], values[i + d]
                values[i], values[i + d] = jnp.maximum(a, b), jnp.minimum(a, b)
        d //= 2
    return values


def over_sublanes(values):
    for shift in (4, 2, 1):
        values = merge_top(values, [pltpu.roll(v, shift, 0) for v in values])
    return values


def kernel(
    test_hbm, fisher_hbm, train_hbm, cand_hbm, rows_ref, out_ref,
    test, fisher, train, cand, gathered, acc, best, sent, homed, tiles,
    send_sem, recv_sem, load_sem,
):
    me, tile = lax.axis_index("train"), lax.axis_index("tile")
    z, y = me // 2, me % 2
    x, core = tile // 2, tile % 2
    q, width = test.shape
    plain, flat = 3 * q // 4, q // 4
    half, flat_half = plain // 2, flat // 2
    flats = 2 * plain
    place = (0, 2, 1, 3)
    order = fisher.shape[1]
    local_rows = train.shape[0]

    inner = (z == 1) | (z == 2)
    outer = (z == 0) | (z == 3)
    flag = ((z + 1) // 2) % 2
    across, two_on = 3 - z, (z + 2) % 4
    zs = [
        z,
        z + 1 - 2 * (z % 2),
        two_on + flag * (across - two_on),
        across + flag * (two_on - across),
    ]
    ys = [y, 1 - y]
    at_tile = [tile, x * 2 + 1 - core, (1 - x) * 2 + core, (1 - x) * 2 + 1 - core]

    def home(a, yr):
        return (zs[a] * 2 + ys[yr], tile)

    def at(t):
        return (me, at_tile[t])

    loads = [
        pltpu.make_async_copy(test_hbm, test, load_sem.at[0]),
        pltpu.make_async_copy(fisher_hbm, fisher, load_sem.at[1]),
        pltpu.make_async_copy(cand_hbm, cand, load_sem.at[2]),
    ]
    for t in range(4):
        start = pl.multiple_of(at_tile[t] * width, width)
        loads.append(pltpu.make_async_copy(
            train_hbm.at[:, pl.ds(start, width)],
            train.at[:, pl.ds(place[t] * width, width)],
            load_sem.at[3 + t],
        ))
    loads[0].start()
    loads[1].start()
    barrier = pltpu.get_barrier_semaphore()
    peers = [home(a, yr) for a in range(4) for yr in range(2) if a or yr]
    peers += [at(t) for t in range(1, 4)]
    for peer in peers:
        pl.semaphore_signal(barrier, inc=1, device_id=peer, device_id_type=MESH)

    homed[...] = jnp.full_like(homed, lowest_score)
    tiles[...] = jnp.full_like(tiles, lowest_score)
    loads[0].wait()
    loads[1].wait()
    for load in loads[2:]:
        load.start()
    for b in range(fisher.shape[0]):
        columns = slice(b * order, (b + 1) * order)
        done = jnp.dot(
            test[:, columns], fisher[b], preferred_element_type=jnp.float32
        ).astype(jnp.bfloat16)
        gathered[0, :plain, columns] = done[:plain]
        gathered[0, flats:flats + flat, columns] = done[plain:]
    pl.semaphore_wait(barrier, len(peers))

    copies = {}

    def copy_to(n, got, source, target, device):
        return pltpu.make_async_remote_copy(
            src_ref=source, dst_ref=target, send_sem=send_sem.at[n], recv_sem=recv_sem.at[got],
            device_id=device, device_id_type=MESH,
        )

    def send(name, source, target, device):
        n = len(copies) + 10
        copies[name] = copy_to(n, n, source, target, device)
        copies[name].start()

    def rows(a, t, start, count):
        return gathered.at[a, pl.ds(start, count), pl.ds(place[t] * width, width)]

    def unit(a):
        return rows(a, 0, 0, plain)

    def plane(a, cr=0):
        return gathered.at[a, pl.ds(flats, 2 * flat), pl.ds(cr * 2 * width, 2 * width)]

    def chain(part, base):
        inner_home = (across * 2 + y, tile)
        return [
            copy_to(base, base + 1, part(0), part(1), home(1, 0)),
            copy_to(base + 1, base + 2, part(0), part(2), inner_home),
            copy_to(base + 2, base + 3, part(1), part(3), inner_home),
            copy_to(base + 3, base + 2, part(2), part(2), home(1, 0)),
            copy_to(base + 4, base + 3, part(3), part(3), home(1, 0)),
        ]

    units, planes = chain(unit, 0), chain(plane, 5)

    def arrived(a):
        copy_to(0, a, unit(0), unit(a), home(1, 0)).wait_recv()

    def plane_arrived(a):
        copy_to(5, 5 + a, plane(0), plane(a), home(1, 0)).wait_recv()

    def plane_first():
        send("cy", rows(0, 0, flats, flat), rows(0, 0, flats + flat, flat), home(0, 1))
        send("cx", rows(0, 0, flats, flat), rows(0, 2, flats, flat), at(2))

    def plane_second():
        copies["cy"].wait_recv()
        other = flats + flat
        send("cx2", rows(0, 0, other, flat_half), rows(0, 2, other, flat_half), at(2))
        copies["cx"].wait_recv()
        send(
            "cy2", rows(0, 2, flats + flat_half, flat_half),
            rows(0, 2, other + flat_half, flat_half), home(0, 1),
        )
        copies["cx2"].wait_recv()
        copies["cy2"].wait_recv()

    def plane_over(a):
        send(("cs", a), plane(a), plane(a, 1), at(1))

    def first(a):
        send(("y", a), rows(a, 0, 0, plain), rows(a, 0, plain, plain), home(0, 1))
        send(("x", a), rows(a, 0, 0, plain), rows(a, 2, 0, plain), at(2))
        send(("s00", a), rows(a, 0, 0, plain), rows(a, 1, 0, plain), at(1))

    def second(a):
        copies["y", a].wait_recv()
        send(("x2", a), rows(a, 0, plain, half), rows(a, 2, plain, half), at(2))
        copies["x", a].wait_recv()
        send(("y2", a), rows(a, 2, half, half), rows(a, 2, plain + half, half), home(0, 1))
        send(("s10", a), rows(a, 0, plain, plain), rows(a, 1, plain, plain), at(1))
        send(("s01", a), rows(a, 2, 0, plain), rows(a, 3, 0, plain), at(1))

    def third(a):
        copies["x2", a].wait_recv()
        copies["y2", a].wait_recv()
        send(("s11", a), rows(a, 2, plain, plain), rows(a, 3, plain, plain), at(1))
        for name in ("s00", "s10", "s01", "s11", "cs"):
            copies[name, a].wait_recv()

    def compute(a):
        part_rows = local_rows // 2

        def multiply(r, carry):
            start = pl.multiple_of(r * part_rows, part_rows)
            chunk = jnp.concatenate([
                gathered[a, :plain], gathered[a, flats:flats + flat],
                gathered[a, plain:flats], gathered[a, flats + flat:],
            ], axis=0)
            part = lax.dot_general(
                train[pl.ds(start, part_rows), :], chunk,
                (((1,), (1,)), ((), ())), preferred_element_type=jnp.float32,
            )
            for g in range(2):
                acc[g, pl.ds(start, part_rows), :] = part[:, g * q:(g + 1) * q]
            return carry

        lax.fori_loop(0, 2, multiply, 0)

        live = rows_ref[0] - tile * local_rows
        step = 8 * TOPK

        def lanes(g, carry):
            best[...] = jnp.full_like(best, lowest_score)

            def block(j, carry):
                base = pl.multiple_of(j * step, step)
                ids = lax.broadcasted_iota(jnp.int32, (8, q), 0) + base
                values = []
                for i in range(TOPK):
                    value = acc[g, pl.ds(base + 8 * i, 8), :]
                    values.append(jnp.where(ids + 8 * i < live, value, lowest_score))
                merged = merge_top([best[i] for i in range(TOPK)], sort_down(values))
                for i in range(TOPK):
                    best[i] = merged[i]
                return carry

            lax.fori_loop(0, local_rows // step, block, 0)
            merged = over_sublanes([best[i] for i in range(TOPK)])
            for i in range(TOPK):
                sent[a, g, i:i + 1, :] = merged[i][0:1]
            return carry

        lax.fori_loop(0, 2, lanes, 0)
        for yr in range(2):
            if a or yr:
                n = len(copies) + 10
                copies["h", a, yr] = copy_to(
                    n, 60 + me, sent.at[a, yr], homed.at[pl.ds(me * TOPK, TOPK)], home(a, yr)
                )
                copies["h", a, yr].start()
            else:
                homed[pl.ds(pl.multiple_of(me * TOPK, TOPK), TOPK)] = sent[0, 0]

    plane_first()
    units[0].start()

    @pl.when(inner)
    def _():
        units[1].start()

    first(0)
    plane_second()
    planes[0].start()

    @pl.when(inner)
    def _():
        planes[1].start()

    plane_over(0)
    arrived(1)

    @pl.when(inner)
    def _():
        units[2].start()
        arrived(2)
        units[3].start()

    first(1)
    second(0)

    @pl.when(inner)
    def _():
        arrived(3)
        units[4].start()

    plane_arrived(1)
    plane_over(1)

    @pl.when(inner)
    def _():
        planes[2].start()
        plane_arrived(2)
        planes[3].start()

    @pl.when(outer)
    def _():
        arrived(2)

    first(2)
    third(0)
    for load in loads[2:]:
        load.wait()
    compute(0)
    second(1)

    @pl.when(inner)
    def _():
        plane_arrived(3)
        planes[4].start()

    @pl.when(outer)
    def _():
        arrived(3)

    first(3)
    third(1)
    compute(1)
    second(2)

    @pl.when(outer)
    def _():
        plane_arrived(2)

    plane_over(2)
    second(3)
    third(2)
    compute(2)

    @pl.when(outer)
    def _():
        plane_arrived(3)

    plane_over(3)
    third(3)
    compute(3)

    for d in range(1, 8):
        source = (me + d) % 8
        copy_to(
            0, 60 + source, sent.at[0, 0], homed.at[pl.ds(source * TOPK, TOPK)], home(0, 1)
        ).wait_recv()
    shard = lax.broadcasted_iota(jnp.int32, (8, q), 0)
    named = shard == cand[0:1, :]
    for c in range(1, cand.shape[0]):
        named = named | (shard == cand[c:c + 1, :])
    merged = over_sublanes([
        jnp.where(named, homed[pl.ds(i, 8, stride=TOPK), :], lowest_score) for i in range(TOPK)
    ])
    for i in range(TOPK):
        tiles[i:i + 1, :] = merged[i][0:1]
    for t in range(1, 4):
        send(("t", t), tiles.at[pl.ds(0, TOPK)], tiles.at[pl.ds(t * TOPK, TOPK)], at(t))
    for t in range(1, 4):
        copies["t", t].wait_recv()
    merged = over_sublanes([tiles[pl.ds(i, 8, stride=TOPK), :] for i in range(TOPK)])
    for i in range(TOPK):
        out_ref[i:i + 1, :] = merged[i][0:1]
    for copy in copies.values():
        copy.wait_send()
    units[0].wait_send()
    planes[0].wait_send()

    @pl.when(inner)
    def _():
        for copy in units[1:] + planes[1:]:
            copy.wait_send()


def fused(test_grads, fisher, train_grads, candidates, shard_rows):
    q, width = test_grads.shape
    local_rows, columns = train_grads.shape
    far = pl.BlockSpec(memory_space=pl.ANY)
    best = pl.pallas_call(
        kernel,
        out_shape=jax.ShapeDtypeStruct((TOPK, q), jnp.float32),
        in_specs=[far] * 4 + [pl.BlockSpec(memory_space=pltpu.SMEM)],
        out_specs=pl.BlockSpec(memory_space=pltpu.VMEM),
        scratch_shapes=[
            pltpu.VMEM(test_grads.shape, jnp.bfloat16),
            pltpu.VMEM(fisher.shape, jnp.bfloat16),
            pltpu.VMEM((local_rows, columns), jnp.bfloat16),
            pltpu.VMEM(candidates.shape[::-1], jnp.int32),
            pltpu.VMEM((4, 2 * q, columns), jnp.bfloat16),
            pltpu.VMEM((2, local_rows, q), jnp.float32),
            pltpu.VMEM((TOPK, 8, q), jnp.float32),
            pltpu.VMEM((4, 2, TOPK, q), jnp.float32),
            pltpu.VMEM((8 * TOPK, q), jnp.float32),
            pltpu.VMEM((8 * TOPK, q), jnp.float32),
            pltpu.SemaphoreType.DMA((68,)),
            pltpu.SemaphoreType.DMA((68,)),
            pltpu.SemaphoreType.DMA((7,)),
        ],
        compiler_params=pltpu.CompilerParams(
            collective_id=0, has_side_effects=True, vmem_limit_bytes=56 * 1024 * 1024
        ),
    )(test_grads, fisher, train_grads, candidates.T, shard_rows)
    return best.T


def solution(mesh):
    placed = (
        P("train", "tile"),
        P("tile", None, None),
        P(("train", "tile"), None),
        P("train", None),
        P("train"),
    )
    sizes = (mesh.shape["train"], mesh.shape["tile"])
    return jax.shard_map(
        fused if sizes == (8, 4) else shards,
        mesh=mesh, in_specs=placed, out_specs=P("train", None), check_vma=False,
    )
```

```python
import functools

import jax
import jax.numpy as jnp
from jax import lax
from jax.experimental import pallas as pl
from jax.experimental.pallas import tpu as pltpu
from jax.sharding import PartitionSpec as P

TOPK = 32
MESH = pl.DeviceIdType.MESH

lowest_score = -1e30


def combined_all(part, axis, combine):
    gathered = lax.all_gather(part, axis)

    def take(source):
        return lax.dynamic_index_in_dim(gathered, source, 0, False)

    return lax.fori_loop(
        1, lax.axis_size(axis), lambda source, state: combine(state, take(source)), take(0)
    )


def combine_leaders(earlier_best, later_best):
    joined = jnp.concatenate([earlier_best, later_best], axis=-1)
    return lax.top_k(joined, earlier_best.shape[-1])[0]


def shards(test_grads, fisher, train_grads, candidates, shard_rows):
    train_count = lax.axis_size("train")
    q_rows, columns = test_grads.shape
    blocks, block_order, _ = fisher.shape
    cand_count = candidates.shape[1]
    local_rows = train_grads.shape[0]
    capacity = max(2, 3 * q_rows * cand_count // (2 * train_count))
    precond = jnp.einsum(
        "qbi,bij->qbj",
        test_grads.reshape(q_rows, blocks, block_order),
        fisher,
        preferred_element_type=jnp.float32,
    )
    precond = precond.reshape(q_rows, columns).astype(jnp.bfloat16)
    targets = candidates.reshape(-1)
    one_hot = (targets[:, None] == jnp.arange(train_count, dtype=jnp.int32)[None, :]).astype(
        jnp.int32
    )
    earlier = jnp.cumsum(one_hot, axis=0) - one_hot
    rank_in = jnp.sum(earlier * one_hot, axis=1)
    slot_index = targets * capacity + rank_in
    sources = jnp.arange(q_rows * cand_count, dtype=jnp.int32) // cand_count
    owner_row = jnp.full((train_count * capacity,), q_rows, jnp.int32).at[slot_index].set(sources)
    row_ids = lax.axis_index("tile") * local_rows + jnp.arange(local_rows, dtype=jnp.int32)
    alive_rows = row_ids < shard_rows[0]
    complete = lax.all_gather(precond, "tile", axis=1, tiled=True)
    padded = jnp.concatenate([complete, jnp.zeros((1, complete.shape[1]), jnp.bfloat16)], axis=0)
    outgoing = padded[owner_row].reshape(train_count, capacity, complete.shape[1])
    scores = jnp.einsum(
        "nck,rk->ncr",
        lax.all_to_all(outgoing, "train", split_axis=0, concat_axis=0, tiled=True),
        train_grads,
        preferred_element_type=jnp.float32,
    )
    masked = jnp.where(alive_rows, scores, lowest_score)
    leaders = lax.top_k(masked, TOPK)[0]
    leaders = combined_all(leaders, "tile", combine_leaders)
    returned = lax.all_to_all(leaders, "train", split_axis=0, concat_axis=0, tiled=True)
    flattened = returned.reshape(train_count * capacity, TOPK)
    per_pair = flattened[slot_index].reshape(q_rows, cand_count * TOPK)
    result_best = lax.top_k(per_pair, TOPK)[0]
    return result_best


def batcher(n):
    pairs = []
    p = 1
    while p < n:
        k = p
        while k >= 1:
            for j in range(k % p, n - k, 2 * k):
                for i in range(min(k, n - j - k)):
                    if (i + j) // (2 * p) == (i + j + k) // (2 * p):
                        pairs.append((i + j, i + j + k))
            k //= 2
        p *= 2
    return pairs


def sort_down(values):
    values = list(values)
    for i, j in batcher(len(values)):
        a, b = values[i], values[j]
        values[i], values[j] = jnp.maximum(a, b), jnp.minimum(a, b)
    return values


def merge_top(first, second):
    n = len(first)
    values = [jnp.maximum(first[i], second[n - 1 - i]) for i in range(n)]
    d = n // 2
    while d >= 1:
        for i in range(n):
            if not i & d:
                a, b = values[i], values[i + d]
                values[i], values[i + d] = jnp.maximum(a, b), jnp.minimum(a, b)
        d //= 2
    return values


def over_sublanes(values):
    for shift in (4, 2, 1):
        values = merge_top(values, [pltpu.roll(v, shift, 0) for v in values])
    return values


def kernel(
    test_hbm, fisher_hbm, train_hbm, cand_hbm, rows_ref, out_ref,
    test, fisher, train, cand, gathered, acc, best, sent, homed, tiles,
    send_sem, recv_sem, load_sem,
):
    me, tile = lax.axis_index("train"), lax.axis_index("tile")
    z, y = me // 2, me % 2
    x, core = tile // 2, tile % 2
    q, width = test.shape
    order = fisher.shape[1]
    local_rows = train.shape[0]
    plain, flat = 3 * width // 4, width // 4
    half, flat_half = plain // 2, flat // 2
    flat_at = [4 * plain + place * flat for place in (0, 2, 1, 3)]

    inner = (z == 1) | (z == 2)
    outer = (z == 0) | (z == 3)
    flag = ((z + 1) // 2) % 2
    across, two_on = 3 - z, (z + 2) % 4
    zs = [
        z,
        z + 1 - 2 * (z % 2),
        two_on + flag * (across - two_on),
        across + flag * (two_on - across),
    ]
    ys = [y, 1 - y]
    at_tile = [tile, x * 2 + 1 - core, (1 - x) * 2 + core, (1 - x) * 2 + 1 - core]

    def home(a, yr):
        return (zs[a] * 2 + ys[yr], tile)

    def at(t):
        return (me, at_tile[t])

    loads = [
        pltpu.make_async_copy(test_hbm, test, load_sem.at[0]),
        pltpu.make_async_copy(fisher_hbm, fisher, load_sem.at[1]),
        pltpu.make_async_copy(cand_hbm, cand, load_sem.at[2]),
    ]
    for t in range(4):
        for skip, count, target in ((0, plain, t * plain), (plain, flat, flat_at[t])):
            start = pl.multiple_of(at_tile[t] * width + skip, 128)
            loads.append(pltpu.make_async_copy(
                train_hbm.at[:, pl.ds(start, count)],
                train.at[:, pl.ds(target, count)],
                load_sem.at[len(loads)],
            ))
    loads[0].start()
    loads[1].start()
    barrier = pltpu.get_barrier_semaphore()
    peers = [home(a, yr) for a in range(4) for yr in range(2) if a or yr]
    peers += [at(t) for t in range(1, 4)]
    for peer in peers:
        pl.semaphore_signal(barrier, inc=1, device_id=peer, device_id_type=MESH)

    homed[...] = jnp.full_like(homed, lowest_score)
    tiles[...] = jnp.full_like(tiles, lowest_score)
    loads[0].wait()
    loads[1].wait()
    for load in loads[2:]:
        load.start()
    for b in range(fisher.shape[0]):
        columns = slice(b * order, (b + 1) * order)
        done = jnp.dot(
            test[:, columns], fisher[b], preferred_element_type=jnp.float32
        ).T.astype(jnp.bfloat16)
        low, cut = b * order, max(0, min(order, plain - b * order))
        if cut:
            gathered[0, 0, low:low + cut] = done[:cut]
        if cut < order:
            begin = flat_at[0] + low + cut - plain
            gathered[0, 0, begin:begin + order - cut] = done[cut:]
    pl.semaphore_wait(barrier, len(peers))

    copies = {}

    def copy_to(n, got, source, target, device):
        return pltpu.make_async_remote_copy(
            src_ref=source, dst_ref=target, send_sem=send_sem.at[n], recv_sem=recv_sem.at[got],
            device_id=device, device_id_type=MESH,
        )

    def send(name, source, target, device):
        n = len(copies) + 10
        copies[name] = copy_to(n, n, source, target, device)
        copies[name].start()

    def rows(a, yr, t, start=0, count=plain):
        return gathered.at[a, yr, pl.ds(t * plain + start, count)]

    def flats(yr, t, start=0, count=flat):
        return gathered.at[0, yr, pl.ds(flat_at[t] + start, count)]

    def unit(a):
        return rows(a, 0, 0)

    def plane(a, cr=0):
        return gathered.at[a, :, pl.ds(4 * plain + cr * 2 * flat, 2 * flat)]

    def chain(part, base):
        inner_home = (across * 2 + y, tile)
        return [
            copy_to(base, base + 1, part(0), part(1), home(1, 0)),
            copy_to(base + 1, base + 2, part(0), part(2), inner_home),
            copy_to(base + 2, base + 3, part(1), part(3), inner_home),
            copy_to(base + 3, base + 2, part(2), part(2), home(1, 0)),
            copy_to(base + 4, base + 3, part(3), part(3), home(1, 0)),
        ]

    units, planes = chain(unit, 0), chain(plane, 5)

    def arrived(a):
        copy_to(0, a, unit(0), unit(a), home(1, 0)).wait_recv()

    def plane_arrived(a):
        copy_to(5, 5 + a, plane(0), plane(a), home(1, 0)).wait_recv()

    def plane_first():
        send("cy", flats(0, 0), flats(1, 0), home(0, 1))
        send("cx", flats(0, 0), flats(0, 2), at(2))

    def plane_second():
        copies["cy"].wait_recv()
        send("cx2", flats(1, 0, 0, flat_half), flats(1, 2, 0, flat_half), at(2))
        copies["cx"].wait_recv()
        send(
            "cy2", flats(0, 2, flat_half, flat_half), flats(1, 2, flat_half, flat_half),
            home(0, 1),
        )
        copies["cx2"].wait_recv()
        copies["cy2"].wait_recv()

    def plane_over(a):
        send(("cs", a), plane(a), plane(a, 1), at(1))

    def first(a):
        send(("y", a), rows(a, 0, 0), rows(a, 1, 0), home(0, 1))
        send(("x", a), rows(a, 0, 0), rows(a, 0, 2), at(2))
        send(("s00", a), rows(a, 0, 0), rows(a, 0, 1), at(1))

    def second(a):
        copies["y", a].wait_recv()
        send(("x2", a), rows(a, 1, 0, 0, half), rows(a, 1, 2, 0, half), at(2))
        copies["x", a].wait_recv()
        send(("y2", a), rows(a, 0, 2, half, half), rows(a, 1, 2, half, half), home(0, 1))
        send(("s10", a), rows(a, 1, 0), rows(a, 1, 1), at(1))
        send(("s01", a), rows(a, 0, 2), rows(a, 0, 3), at(1))

    def third(a):
        copies["x2", a].wait_recv()
        copies["y2", a].wait_recv()
        send(("s11", a), rows(a, 1, 2), rows(a, 1, 3), at(1))
        for name in ("s00", "s10", "s01", "s11", "cs"):
            copies[name, a].wait_recv()

    def compute(a):
        part_rows = local_rows // 2

        def multiply(r, carry):
            start = pl.multiple_of(r * part_rows, part_rows)
            part = jnp.dot(
                train[pl.ds(start, part_rows), :],
                jnp.concatenate([gathered[a, 0], gathered[a, 1]], axis=1),
                preferred_element_type=jnp.float32,
            )
            for g in range(2):
                acc[g, pl.ds(start, part_rows), :] = part[:, g * q:(g + 1) * q]
            return carry

        lax.fori_loop(0, 2, multiply, 0)

        live = rows_ref[0] - tile * local_rows
        step = 8 * TOPK

        def lanes(g, carry):
            def ordered(j):
                base = pl.multiple_of(j * step, step)
                ids = lax.broadcasted_iota(jnp.int32, (8, q), 0) + base
                values = []
                for i in range(TOPK):
                    value = acc[g, pl.ds(base + 8 * i, 8), :]
                    values.append(jnp.where(ids + 8 * i < live, value, lowest_score))
                return sort_down(values)

            def keep(values):
                for i in range(TOPK):
                    best[i] = values[i]

            def block(j, carry):
                keep(merge_top([best[i] for i in range(TOPK)], ordered(j)))
                return carry

            keep(ordered(0))
            lax.fori_loop(1, local_rows // step, block, 0)
            merged = over_sublanes([best[i] for i in range(TOPK)])
            for i in range(TOPK):
                sent[a, g, i:i + 1, :] = merged[i][0:1]
            return carry

        lax.fori_loop(0, 2, lanes, 0)
        for yr in range(2):
            if a or yr:
                n = len(copies) + 10
                copies["h", a, yr] = copy_to(
                    n, 60 + me, sent.at[a, yr], homed.at[pl.ds(me * TOPK, TOPK)], home(a, yr)
                )
                copies["h", a, yr].start()
            else:
                homed[pl.ds(pl.multiple_of(me * TOPK, TOPK), TOPK)] = sent[0, 0]

    plane_first()
    units[0].start()

    @pl.when(inner)
    def _():
        units[1].start()

    first(0)
    plane_second()
    planes[0].start()

    @pl.when(inner)
    def _():
        planes[1].start()

    plane_over(0)
    arrived(1)

    @pl.when(inner)
    def _():
        units[2].start()
        arrived(2)
        units[3].start()

    first(1)
    second(0)

    @pl.when(inner)
    def _():
        arrived(3)
        units[4].start()

    plane_arrived(1)
    plane_over(1)

    @pl.when(inner)
    def _():
        planes[2].start()
        plane_arrived(2)
        planes[3].start()

    @pl.when(outer)
    def _():
        arrived(2)

    first(2)
    third(0)
    for load in loads[2:]:
        load.wait()
    compute(0)
    second(1)

    @pl.when(inner)
    def _():
        plane_arrived(3)
        planes[4].start()

    @pl.when(outer)
    def _():
        arrived(3)

    first(3)
    third(1)
    compute(1)
    second(2)

    @pl.when(outer)
    def _():
        plane_arrived(2)

    plane_over(2)
    second(3)
    third(2)
    compute(2)

    @pl.when(outer)
    def _():
        plane_arrived(3)

    plane_over(3)
    third(3)
    compute(3)

    for d in range(1, 8):
        source = (me + d) % 8
        copy_to(
            0, 60 + source, sent.at[0, 0], homed.at[pl.ds(source * TOPK, TOPK)], home(0, 1)
        ).wait_recv()
    shard = lax.broadcasted_iota(jnp.int32, (8, q), 0)
    named = shard == cand[0:1, :]
    for c in range(1, cand.shape[0]):
        named = named | (shard == cand[c:c + 1, :])
    merged = over_sublanes([
        jnp.where(named, homed[pl.ds(i, 8, stride=TOPK), :], lowest_score) for i in range(TOPK)
    ])
    for i in range(TOPK):
        tiles[i:i + 1, :] = merged[i][0:1]
    for t in range(1, 4):
        send(("t", t), tiles.at[pl.ds(0, TOPK)], tiles.at[pl.ds(t * TOPK, TOPK)], at(t))
    for t in range(1, 4):
        copies["t", t].wait_recv()
    merged = over_sublanes([tiles[pl.ds(i, 8, stride=TOPK), :] for i in range(TOPK)])
    for i in range(TOPK):
        out_ref[i:i + 1, :] = merged[i][0:1]
    for copy in copies.values():
        copy.wait_send()
    units[0].wait_send()
    planes[0].wait_send()

    @pl.when(inner)
    def _():
        for copy in units[1:] + planes[1:]:
            copy.wait_send()


def fused(test_grads, fisher, train_grads, candidates, shard_rows):
    q, width = test_grads.shape
    local_rows, columns = train_grads.shape
    far = pl.BlockSpec(memory_space=pl.ANY)
    best = pl.pallas_call(
        kernel,
        out_shape=jax.ShapeDtypeStruct((TOPK, q), jnp.float32),
        in_specs=[far] * 4 + [pl.BlockSpec(memory_space=pltpu.SMEM)],
        out_specs=pl.BlockSpec(memory_space=pltpu.VMEM),
        scratch_shapes=[
            pltpu.VMEM(test_grads.shape, jnp.bfloat16),
            pltpu.VMEM(fisher.shape, jnp.bfloat16),
            pltpu.VMEM((local_rows, columns), jnp.bfloat16),
            pltpu.VMEM(candidates.shape[::-1], jnp.int32),
            pltpu.VMEM((4, 2, columns, q), jnp.bfloat16),
            pltpu.VMEM((2, local_rows, q), jnp.float32),
            pltpu.VMEM((TOPK, 8, q), jnp.float32),
            pltpu.VMEM((4, 2, TOPK, q), jnp.float32),
            pltpu.VMEM((8 * TOPK, q), jnp.float32),
            pltpu.VMEM((8 * TOPK, q), jnp.float32),
            pltpu.SemaphoreType.DMA((68,)),
            pltpu.SemaphoreType.DMA((68,)),
            pltpu.SemaphoreType.DMA((11,)),
        ],
        compiler_params=pltpu.CompilerParams(
            collective_id=0, has_side_effects=True, vmem_limit_bytes=56 * 1024 * 1024
        ),
    )(test_grads, fisher, train_grads, candidates.T, shard_rows)
    return best.T


def solution(mesh):
    placed = (
        P("train", "tile"),
        P("tile", None, None),
        P(("train", "tile"), None),
        P("train", None),
        P("train"),
    )
    sizes = (mesh.shape["train"], mesh.shape["tile"])
    return jax.shard_map(
        fused if sizes == (8, 4) else shards,
        mesh=mesh, in_specs=placed, out_specs=P("train", None), check_vma=False,
    )
```

```python
import functools

import jax
import jax.numpy as jnp
from jax import lax
from jax.experimental import pallas as pl
from jax.experimental.pallas import tpu as pltpu
from jax.sharding import PartitionSpec as P

TOPK = 32
MESH = pl.DeviceIdType.MESH

lowest_score = -1e30


def combined_all(part, axis, combine):
    gathered = lax.all_gather(part, axis)

    def take(source):
        return lax.dynamic_index_in_dim(gathered, source, 0, False)

    return lax.fori_loop(
        1, lax.axis_size(axis), lambda source, state: combine(state, take(source)), take(0)
    )


def combine_leaders(earlier_best, later_best):
    joined = jnp.concatenate([earlier_best, later_best], axis=-1)
    return lax.top_k(joined, earlier_best.shape[-1])[0]


def shards(test_grads, fisher, train_grads, candidates, shard_rows):
    train_count = lax.axis_size("train")
    q_rows, columns = test_grads.shape
    blocks, block_order, _ = fisher.shape
    cand_count = candidates.shape[1]
    local_rows = train_grads.shape[0]
    capacity = max(2, 3 * q_rows * cand_count // (2 * train_count))
    precond = jnp.einsum(
        "qbi,bij->qbj",
        test_grads.reshape(q_rows, blocks, block_order),
        fisher,
        preferred_element_type=jnp.float32,
    )
    precond = precond.reshape(q_rows, columns).astype(jnp.bfloat16)
    targets = candidates.reshape(-1)
    one_hot = (targets[:, None] == jnp.arange(train_count, dtype=jnp.int32)[None, :]).astype(
        jnp.int32
    )
    earlier = jnp.cumsum(one_hot, axis=0) - one_hot
    rank_in = jnp.sum(earlier * one_hot, axis=1)
    slot_index = targets * capacity + rank_in
    sources = jnp.arange(q_rows * cand_count, dtype=jnp.int32) // cand_count
    owner_row = jnp.full((train_count * capacity,), q_rows, jnp.int32).at[slot_index].set(sources)
    row_ids = lax.axis_index("tile") * local_rows + jnp.arange(local_rows, dtype=jnp.int32)
    alive_rows = row_ids < shard_rows[0]
    complete = lax.all_gather(precond, "tile", axis=1, tiled=True)
    padded = jnp.concatenate([complete, jnp.zeros((1, complete.shape[1]), jnp.bfloat16)], axis=0)
    outgoing = padded[owner_row].reshape(train_count, capacity, complete.shape[1])
    scores = jnp.einsum(
        "nck,rk->ncr",
        lax.all_to_all(outgoing, "train", split_axis=0, concat_axis=0, tiled=True),
        train_grads,
        preferred_element_type=jnp.float32,
    )
    masked = jnp.where(alive_rows, scores, lowest_score)
    leaders = lax.top_k(masked, TOPK)[0]
    leaders = combined_all(leaders, "tile", combine_leaders)
    returned = lax.all_to_all(leaders, "train", split_axis=0, concat_axis=0, tiled=True)
    flattened = returned.reshape(train_count * capacity, TOPK)
    per_pair = flattened[slot_index].reshape(q_rows, cand_count * TOPK)
    result_best = lax.top_k(per_pair, TOPK)[0]
    return result_best


def batcher(n):
    pairs = []
    p = 1
    while p < n:
        k = p
        while k >= 1:
            for j in range(k % p, n - k, 2 * k):
                for i in range(min(k, n - j - k)):
                    if (i + j) // (2 * p) == (i + j + k) // (2 * p):
                        pairs.append((i + j, i + j + k))
            k //= 2
        p *= 2
    return pairs


def sort_down(values):
    values = list(values)
    for i, j in batcher(len(values)):
        a, b = values[i], values[j]
        values[i], values[j] = jnp.maximum(a, b), jnp.minimum(a, b)
    return values


def merge_top(first, second):
    n = len(first)
    values = [jnp.maximum(first[i], second[n - 1 - i]) for i in range(n)]
    d = n // 2
    while d >= 1:
        for i in range(n):
            if not i & d:
                a, b = values[i], values[i + d]
                values[i], values[i + d] = jnp.maximum(a, b), jnp.minimum(a, b)
        d //= 2
    return values


def over_sublanes(values):
    for shift in (4, 2, 1):
        values = merge_top(values, [pltpu.roll(v, shift, 0) for v in values])
    return values


def kernel(
    test_hbm, fisher_hbm, train_hbm, cand_hbm, rows_ref, out_ref,
    test, fisher, train, cand, gathered, acc, best, sent, homed, tiles,
    send_sem, recv_sem, load_sem,
):
    me, tile = lax.axis_index("train"), lax.axis_index("tile")
    z, y = me // 2, me % 2
    x, core = tile // 2, tile % 2
    q, width = test.shape
    order = fisher.shape[1]
    local_rows = train.shape[0]
    plain, flat = 3 * width // 4, width // 4
    half, flat_half = plain // 2, flat // 2
    flat_at = [4 * plain + place * flat for place in (0, 2, 1, 3)]

    inner = (z == 1) | (z == 2)
    outer = (z == 0) | (z == 3)
    flag = ((z + 1) // 2) % 2
    across, two_on = 3 - z, (z + 2) % 4
    zs = [
        z,
        z + 1 - 2 * (z % 2),
        two_on + flag * (across - two_on),
        across + flag * (two_on - across),
    ]
    ys = [y, 1 - y]
    at_tile = [tile, x * 2 + 1 - core, (1 - x) * 2 + core, (1 - x) * 2 + 1 - core]

    def home(a, yr):
        return (zs[a] * 2 + ys[yr], tile)

    def at(t):
        return (me, at_tile[t])

    loads = [
        pltpu.make_async_copy(test_hbm, test, load_sem.at[0]),
        pltpu.make_async_copy(fisher_hbm, fisher, load_sem.at[1]),
        pltpu.make_async_copy(cand_hbm, cand, load_sem.at[2]),
    ]
    for t in range(4):
        for skip, count, target in ((0, plain, t * plain), (plain, flat, flat_at[t])):
            start = pl.multiple_of(at_tile[t] * width + skip, 128)
            loads.append(pltpu.make_async_copy(
                train_hbm.at[:, pl.ds(start, count)],
                train.at[:, pl.ds(target, count)],
                load_sem.at[len(loads)],
            ))
    loads[0].start()
    loads[1].start()
    barrier = pltpu.get_barrier_semaphore()
    peers = [home(a, yr) for a in range(4) for yr in range(2) if a or yr]
    peers += [at(t) for t in range(1, 4)]
    for peer in peers:
        pl.semaphore_signal(barrier, inc=1, device_id=peer, device_id_type=MESH)

    homed[...] = jnp.full_like(homed, lowest_score)
    tiles[...] = jnp.full_like(tiles, lowest_score)
    loads[0].wait()
    loads[1].wait()
    for load in loads[2:]:
        load.start()
    for b in range(fisher.shape[0]):
        columns = slice(b * order, (b + 1) * order)
        done = jnp.dot(
            test[:, columns], fisher[b], preferred_element_type=jnp.float32
        ).T.astype(jnp.bfloat16)
        low, cut = b * order, max(0, min(order, plain - b * order))
        if cut:
            gathered[0, 0, low:low + cut] = done[:cut]
        if cut < order:
            begin = flat_at[0] + low + cut - plain
            gathered[0, 0, begin:begin + order - cut] = done[cut:]
    pl.semaphore_wait(barrier, len(peers))

    copies = {}

    def copy_to(n, got, source, target, device):
        return pltpu.make_async_remote_copy(
            src_ref=source, dst_ref=target, send_sem=send_sem.at[n], recv_sem=recv_sem.at[got],
            device_id=device, device_id_type=MESH,
        )

    def send(name, source, target, device):
        n = len(copies) + 10
        copies[name] = copy_to(n, n, source, target, device)
        copies[name].start()

    def rows(a, yr, t, start=0, count=plain):
        return gathered.at[a, yr, pl.ds(t * plain + start, count)]

    def flats(yr, t, start=0, count=flat):
        return gathered.at[0, yr, pl.ds(flat_at[t] + start, count)]

    def unit(a):
        return rows(a, 0, 0)

    def plane(a, cr=0):
        return gathered.at[a, :, pl.ds(4 * plain + cr * 2 * flat, 2 * flat)]

    def chain(part, base):
        inner_home = (across * 2 + y, tile)
        return [
            copy_to(base, base + 1, part(0), part(1), home(1, 0)),
            copy_to(base + 1, base + 2, part(0), part(2), inner_home),
            copy_to(base + 2, base + 3, part(1), part(3), inner_home),
            copy_to(base + 3, base + 2, part(2), part(2), home(1, 0)),
            copy_to(base + 4, base + 3, part(3), part(3), home(1, 0)),
        ]

    units, planes = chain(unit, 0), chain(plane, 5)

    def arrived(a):
        copy_to(0, a, unit(0), unit(a), home(1, 0)).wait_recv()

    def plane_arrived(a):
        copy_to(5, 5 + a, plane(0), plane(a), home(1, 0)).wait_recv()

    def plane_first():
        send("cy", flats(0, 0), flats(1, 0), home(0, 1))
        send("cx", flats(0, 0), flats(0, 2), at(2))

    def plane_second():
        copies["cy"].wait_recv()
        send("cx2", flats(1, 0, 0, flat_half), flats(1, 2, 0, flat_half), at(2))
        copies["cx"].wait_recv()
        send(
            "cy2", flats(0, 2, flat_half, flat_half), flats(1, 2, flat_half, flat_half),
            home(0, 1),
        )

    def plane_third():
        copies["cx2"].wait_recv()
        copies["cy2"].wait_recv()

    def plane_over(a):
        send(("cs", a), plane(a), plane(a, 1), at(1))

    def first(a):
        send(("y", a), rows(a, 0, 0), rows(a, 1, 0), home(0, 1))
        send(("x", a), rows(a, 0, 0), rows(a, 0, 2), at(2))
        send(("s00", a), rows(a, 0, 0), rows(a, 0, 1), at(1))

    def second(a):
        copies["y", a].wait_recv()
        send(("x2", a), rows(a, 1, 0, 0, half), rows(a, 1, 2, 0, half), at(2))
        copies["x", a].wait_recv()
        send(("y2", a), rows(a, 0, 2, half, half), rows(a, 1, 2, half, half), home(0, 1))
        send(("s10", a), rows(a, 1, 0), rows(a, 1, 1), at(1))
        send(("s01", a), rows(a, 0, 2), rows(a, 0, 3), at(1))

    def third(a):
        copies["x2", a].wait_recv()
        copies["y2", a].wait_recv()
        send(("s11", a), rows(a, 1, 2), rows(a, 1, 3), at(1))
        for name in ("s00", "s10", "s01", "s11"):
            copies[name, a].wait_recv()

    def compute(a):
        part_rows = local_rows // 2

        def multiply(low, high):
            def rows_of(r, carry):
                start = pl.multiple_of(r * part_rows, part_rows)
                part = jnp.dot(
                    train[pl.ds(start, part_rows), low:high],
                    jnp.concatenate([gathered[a, 0, low:high], gathered[a, 1, low:high]], axis=1),
                    preferred_element_type=jnp.float32,
                )
                for g in range(2):
                    block = part[:, g * q:(g + 1) * q]
                    if low:
                        block = block + acc[g, pl.ds(start, part_rows), :]
                    acc[g, pl.ds(start, part_rows), :] = block
                return carry

            lax.fori_loop(0, 2, rows_of, 0)

        if a == 3:
            multiply(0, 4 * plain)
            copies["cs", a].wait_recv()
            multiply(4 * plain, 4 * width)
        else:
            copies["cs", a].wait_recv()
            multiply(0, 4 * width)

        live = rows_ref[0] - tile * local_rows
        step = 8 * TOPK

        def lanes(g, carry):
            def ordered(j):
                base = pl.multiple_of(j * step, step)
                ids = lax.broadcasted_iota(jnp.int32, (8, q), 0) + base
                values = []
                for i in range(TOPK):
                    value = acc[g, pl.ds(base + 8 * i, 8), :]
                    values.append(jnp.where(ids + 8 * i < live, value, lowest_score))
                return sort_down(values)

            def keep(values):
                for i in range(TOPK):
                    best[i] = values[i]

            def block(j, carry):
                keep(merge_top([best[i] for i in range(TOPK)], ordered(j)))
                return carry

            keep(ordered(0))
            lax.fori_loop(1, local_rows // step, block, 0)
            merged = over_sublanes([best[i] for i in range(TOPK)])
            for i in range(TOPK):
                sent[a, g, i:i + 1, :] = merged[i][0:1]
            return carry

        lax.fori_loop(0, 2, lanes, 0)
        for yr in range(2):
            if a or yr:
                n = len(copies) + 10
                copies["h", a, yr] = copy_to(
                    n, 60 + me, sent.at[a, yr], homed.at[pl.ds(me * TOPK, TOPK)], home(a, yr)
                )
                copies["h", a, yr].start()
            else:
                homed[pl.ds(pl.multiple_of(me * TOPK, TOPK), TOPK)] = sent[0, 0]

    plane_first()
    units[0].start()

    @pl.when(inner)
    def _():
        units[1].start()

    plane_second()
    first(0)
    plane_third()
    planes[0].start()

    @pl.when(inner)
    def _():
        planes[1].start()

    plane_over(0)
    arrived(1)

    @pl.when(inner)
    def _():
        units[2].start()
        arrived(2)
        units[3].start()

    first(1)
    second(0)

    @pl.when(inner)
    def _():
        arrived(3)
        units[4].start()

    plane_arrived(1)
    plane_over(1)

    @pl.when(inner)
    def _():
        planes[2].start()
        plane_arrived(2)
        planes[3].start()

    @pl.when(outer)
    def _():
        arrived(2)

    first(2)
    third(0)
    for load in loads[2:]:
        load.wait()
    compute(0)
    second(1)

    @pl.when(inner)
    def _():
        plane_arrived(3)
        planes[4].start()

    @pl.when(outer)
    def _():
        arrived(3)

    first(3)
    third(1)
    compute(1)
    second(2)

    @pl.when(outer)
    def _():
        plane_arrived(2)

    plane_over(2)
    second(3)
    third(2)
    compute(2)

    @pl.when(outer)
    def _():
        plane_arrived(3)

    plane_over(3)
    third(3)
    compute(3)

    for d in range(1, 8):
        source = (me + d) % 8
        copy_to(
            0, 60 + source, sent.at[0, 0], homed.at[pl.ds(source * TOPK, TOPK)], home(0, 1)
        ).wait_recv()
    shard = lax.broadcasted_iota(jnp.int32, (8, q), 0)
    named = shard == cand[0:1, :]
    for c in range(1, cand.shape[0]):
        named = named | (shard == cand[c:c + 1, :])
    merged = over_sublanes([
        jnp.where(named, homed[pl.ds(i, 8, stride=TOPK), :], lowest_score) for i in range(TOPK)
    ])
    for i in range(TOPK):
        tiles[i:i + 1, :] = merged[i][0:1]
    for t in range(1, 4):
        send(("t", t), tiles.at[pl.ds(0, TOPK)], tiles.at[pl.ds(t * TOPK, TOPK)], at(t))
    for t in range(1, 4):
        copies["t", t].wait_recv()
    merged = over_sublanes([tiles[pl.ds(i, 8, stride=TOPK), :] for i in range(TOPK)])
    for i in range(TOPK):
        out_ref[i:i + 1, :] = merged[i][0:1]
    for copy in copies.values():
        copy.wait_send()
    units[0].wait_send()
    planes[0].wait_send()

    @pl.when(inner)
    def _():
        for copy in units[1:] + planes[1:]:
            copy.wait_send()


def fused(test_grads, fisher, train_grads, candidates, shard_rows):
    q, width = test_grads.shape
    local_rows, columns = train_grads.shape
    far = pl.BlockSpec(memory_space=pl.ANY)
    best = pl.pallas_call(
        kernel,
        out_shape=jax.ShapeDtypeStruct((TOPK, q), jnp.float32),
        in_specs=[far] * 4 + [pl.BlockSpec(memory_space=pltpu.SMEM)],
        out_specs=pl.BlockSpec(memory_space=pltpu.VMEM),
        scratch_shapes=[
            pltpu.VMEM(test_grads.shape, jnp.bfloat16),
            pltpu.VMEM(fisher.shape, jnp.bfloat16),
            pltpu.VMEM((local_rows, columns), jnp.bfloat16),
            pltpu.VMEM(candidates.shape[::-1], jnp.int32),
            pltpu.VMEM((4, 2, columns, q), jnp.bfloat16),
            pltpu.VMEM((2, local_rows, q), jnp.float32),
            pltpu.VMEM((TOPK, 8, q), jnp.float32),
            pltpu.VMEM((4, 2, TOPK, q), jnp.float32),
            pltpu.VMEM((8 * TOPK, q), jnp.float32),
            pltpu.VMEM((8 * TOPK, q), jnp.float32),
            pltpu.SemaphoreType.DMA((68,)),
            pltpu.SemaphoreType.DMA((68,)),
            pltpu.SemaphoreType.DMA((11,)),
        ],
        compiler_params=pltpu.CompilerParams(
            collective_id=0, has_side_effects=True, vmem_limit_bytes=56 * 1024 * 1024
        ),
    )(test_grads, fisher, train_grads, candidates.T, shard_rows)
    return best.T


def solution(mesh):
    placed = (
        P("train", "tile"),
        P("tile", None, None),
        P(("train", "tile"), None),
        P("train", None),
        P("train"),
    )
    sizes = (mesh.shape["train"], mesh.shape["tile"])
    return jax.shard_map(
        fused if sizes == (8, 4) else shards,
        mesh=mesh, in_specs=placed, out_specs=P("train", None), check_vma=False,
    )
```

```python
import functools

import jax
import jax.numpy as jnp
from jax import lax
from jax.experimental import pallas as pl
from jax.experimental.pallas import tpu as pltpu
from jax.sharding import PartitionSpec as P

TOPK = 32
MESH = pl.DeviceIdType.MESH

lowest_score = -1e30


def combined_all(part, axis, combine):
    gathered = lax.all_gather(part, axis)

    def take(source):
        return lax.dynamic_index_in_dim(gathered, source, 0, False)

    return lax.fori_loop(
        1, lax.axis_size(axis), lambda source, state: combine(state, take(source)), take(0)
    )


def combine_leaders(earlier_best, later_best):
    joined = jnp.concatenate([earlier_best, later_best], axis=-1)
    return lax.top_k(joined, earlier_best.shape[-1])[0]


def shards(test_grads, fisher, train_grads, candidates, shard_rows):
    train_count = lax.axis_size("train")
    q_rows, columns = test_grads.shape
    blocks, block_order, _ = fisher.shape
    cand_count = candidates.shape[1]
    local_rows = train_grads.shape[0]
    capacity = max(2, 3 * q_rows * cand_count // (2 * train_count))
    precond = jnp.einsum(
        "qbi,bij->qbj",
        test_grads.reshape(q_rows, blocks, block_order),
        fisher,
        preferred_element_type=jnp.float32,
    )
    precond = precond.reshape(q_rows, columns).astype(jnp.bfloat16)
    targets = candidates.reshape(-1)
    one_hot = (targets[:, None] == jnp.arange(train_count, dtype=jnp.int32)[None, :]).astype(
        jnp.int32
    )
    earlier = jnp.cumsum(one_hot, axis=0) - one_hot
    rank_in = jnp.sum(earlier * one_hot, axis=1)
    slot_index = targets * capacity + rank_in
    sources = jnp.arange(q_rows * cand_count, dtype=jnp.int32) // cand_count
    owner_row = jnp.full((train_count * capacity,), q_rows, jnp.int32).at[slot_index].set(sources)
    row_ids = lax.axis_index("tile") * local_rows + jnp.arange(local_rows, dtype=jnp.int32)
    alive_rows = row_ids < shard_rows[0]
    complete = lax.all_gather(precond, "tile", axis=1, tiled=True)
    padded = jnp.concatenate([complete, jnp.zeros((1, complete.shape[1]), jnp.bfloat16)], axis=0)
    outgoing = padded[owner_row].reshape(train_count, capacity, complete.shape[1])
    scores = jnp.einsum(
        "nck,rk->ncr",
        lax.all_to_all(outgoing, "train", split_axis=0, concat_axis=0, tiled=True),
        train_grads,
        preferred_element_type=jnp.float32,
    )
    masked = jnp.where(alive_rows, scores, lowest_score)
    leaders = lax.top_k(masked, TOPK)[0]
    leaders = combined_all(leaders, "tile", combine_leaders)
    returned = lax.all_to_all(leaders, "train", split_axis=0, concat_axis=0, tiled=True)
    flattened = returned.reshape(train_count * capacity, TOPK)
    per_pair = flattened[slot_index].reshape(q_rows, cand_count * TOPK)
    result_best = lax.top_k(per_pair, TOPK)[0]
    return result_best


def batcher(n):
    pairs = []
    p = 1
    while p < n:
        k = p
        while k >= 1:
            for j in range(k % p, n - k, 2 * k):
                for i in range(min(k, n - j - k)):
                    if (i + j) // (2 * p) == (i + j + k) // (2 * p):
                        pairs.append((i + j, i + j + k))
            k //= 2
        p *= 2
    return pairs


def sort_down(values):
    values = list(values)
    for i, j in batcher(len(values)):
        a, b = values[i], values[j]
        values[i], values[j] = jnp.maximum(a, b), jnp.minimum(a, b)
    return values


def merge_top(first, second):
    n = len(first)
    values = [jnp.maximum(first[i], second[n - 1 - i]) for i in range(n)]
    d = n // 2
    while d >= 1:
        for i in range(n):
            if not i & d:
                a, b = values[i], values[i + d]
                values[i], values[i + d] = jnp.maximum(a, b), jnp.minimum(a, b)
        d //= 2
    return values


def over_sublanes(values):
    for shift in (4, 2, 1):
        values = merge_top(values, [pltpu.roll(v, shift, 0) for v in values])
    return values


def kernel(
    test_hbm, fisher_hbm, train_hbm, cand_hbm, rows_ref, out_ref,
    test, fisher, train, cand, gathered, acc, best, sent, homed, tiles,
    send_sem, recv_sem, load_sem,
):
    me, tile = lax.axis_index("train"), lax.axis_index("tile")
    z, y = me // 2, me % 2
    x, core = tile // 2, tile % 2
    q, width = test.shape
    order = fisher.shape[1]
    local_rows = train.shape[0]
    plain, flat = 3 * width // 4, width // 4
    half, flat_half = plain // 2, flat // 2
    flat_at = [4 * plain + place * flat for place in (0, 2, 1, 3)]

    inner = (z == 1) | (z == 2)
    outer = (z == 0) | (z == 3)
    flag = ((z + 1) // 2) % 2
    across, two_on = 3 - z, (z + 2) % 4
    zs = [
        z,
        z + 1 - 2 * (z % 2),
        two_on + flag * (across - two_on),
        across + flag * (two_on - across),
    ]
    ys = [y, 1 - y]
    at_tile = [tile, x * 2 + 1 - core, (1 - x) * 2 + core, (1 - x) * 2 + 1 - core]

    def home(a, yr):
        return (zs[a] * 2 + ys[yr], tile)

    def at(t):
        return (me, at_tile[t])

    loads = [
        pltpu.make_async_copy(test_hbm, test, load_sem.at[0]),
        pltpu.make_async_copy(fisher_hbm, fisher, load_sem.at[1]),
        pltpu.make_async_copy(cand_hbm, cand, load_sem.at[2]),
    ]
    for t in range(4):
        for skip, count, target in ((0, plain, t * plain), (plain, flat, flat_at[t])):
            start = pl.multiple_of(at_tile[t] * width + skip, 128)
            loads.append(pltpu.make_async_copy(
                train_hbm.at[:, pl.ds(start, count)],
                train.at[:, pl.ds(target, count)],
                load_sem.at[len(loads)],
            ))
    loads[0].start()
    loads[1].start()
    barrier = pltpu.get_barrier_semaphore()
    peers = [home(a, yr) for a in range(4) for yr in range(2) if a or yr]
    peers += [at(t) for t in range(1, 4)]
    for peer in peers:
        pl.semaphore_signal(barrier, inc=1, device_id=peer, device_id_type=MESH)

    homed[...] = jnp.full_like(homed, lowest_score)
    tiles[...] = jnp.full_like(tiles, lowest_score)
    loads[0].wait()
    loads[1].wait()
    for load in loads[2:]:
        load.start()
    for b in range(fisher.shape[0]):
        columns = slice(b * order, (b + 1) * order)
        done = jnp.dot(
            test[:, columns], fisher[b], preferred_element_type=jnp.float32
        ).T.astype(jnp.bfloat16)
        low, cut = b * order, max(0, min(order, plain - b * order))
        if cut:
            gathered[0, 0, low:low + cut] = done[:cut]
        if cut < order:
            begin = flat_at[0] + low + cut - plain
            gathered[0, 0, begin:begin + order - cut] = done[cut:]
    pl.semaphore_wait(barrier, len(peers))

    copies = {}

    def copy_to(n, got, source, target, device):
        return pltpu.make_async_remote_copy(
            src_ref=source, dst_ref=target, send_sem=send_sem.at[n], recv_sem=recv_sem.at[got],
            device_id=device, device_id_type=MESH,
        )

    def send(name, source, target, device):
        n = len(copies) + 10
        copies[name] = copy_to(n, n, source, target, device)
        copies[name].start()

    def rows(a, yr, t, start=0, count=plain):
        return gathered.at[a, yr, pl.ds(t * plain + start, count)]

    def flats(yr, t, start=0, count=flat):
        return gathered.at[0, yr, pl.ds(flat_at[t] + start, count)]

    def unit(a):
        return rows(a, 0, 0)

    def plane(a, cr=0):
        return gathered.at[a, :, pl.ds(4 * plain + cr * 2 * flat, 2 * flat)]

    def chain(part, base):
        inner_home = (across * 2 + y, tile)
        return [
            copy_to(base, base + 1, part(0), part(1), home(1, 0)),
            copy_to(base + 1, base + 2, part(0), part(2), inner_home),
            copy_to(base + 2, base + 3, part(1), part(3), inner_home),
            copy_to(base + 3, base + 2, part(2), part(2), home(1, 0)),
            copy_to(base + 4, base + 3, part(3), part(3), home(1, 0)),
        ]

    units, planes = chain(unit, 0), chain(plane, 5)

    def arrived(a):
        copy_to(0, a, unit(0), unit(a), home(1, 0)).wait_recv()

    def plane_arrived(a):
        copy_to(5, 5 + a, plane(0), plane(a), home(1, 0)).wait_recv()

    def plane_first():
        send("cy", flats(0, 0), flats(1, 0), home(0, 1))
        send("cx", flats(0, 0), flats(0, 2), at(2))

    def plane_second():
        copies["cy"].wait_recv()
        send("cx2", flats(1, 0, 0, flat_half), flats(1, 2, 0, flat_half), at(2))
        copies["cx"].wait_recv()
        send(
            "cy2", flats(0, 2, flat_half, flat_half), flats(1, 2, flat_half, flat_half),
            home(0, 1),
        )

    def plane_third():
        copies["cx2"].wait_recv()
        copies["cy2"].wait_recv()

    def plane_over(a):
        send(("cs", a), plane(a), plane(a, 1), at(1))

    def first(a):
        send(("y", a), rows(a, 0, 0), rows(a, 1, 0), home(0, 1))
        send(("x", a), rows(a, 0, 0), rows(a, 0, 2), at(2))
        send(("s00", a), rows(a, 0, 0), rows(a, 0, 1), at(1))

    def second(a):
        copies["y", a].wait_recv()
        send(("x2", a), rows(a, 1, 0, 0, half), rows(a, 1, 2, 0, half), at(2))
        copies["x", a].wait_recv()
        send(("y2", a), rows(a, 0, 2, half, half), rows(a, 1, 2, half, half), home(0, 1))
        send(("s10", a), rows(a, 1, 0), rows(a, 1, 1), at(1))
        send(("s01", a), rows(a, 0, 2), rows(a, 0, 3), at(1))

    def third(a):
        copies["x2", a].wait_recv()
        copies["y2", a].wait_recv()
        send(("s11", a), rows(a, 1, 2), rows(a, 1, 3), at(1))
        for name in ("s00", "s10", "s01", "s11"):
            copies[name, a].wait_recv()

    def compute(a):
        part_rows = local_rows

        def multiply(low, high):
            def rows_of(r, carry):
                start = r * part_rows
                part = jnp.dot(
                    train[pl.ds(start, part_rows), low:high],
                    jnp.concatenate([gathered[a, 0, low:high], gathered[a, 1, low:high]], axis=1),
                    preferred_element_type=jnp.float32,
                )
                for g in range(2):
                    block = part[:, g * q:(g + 1) * q]
                    if low:
                        block = block + acc[g, pl.ds(start, part_rows), :]
                    acc[g, pl.ds(start, part_rows), :] = block
                return carry

            rows_of(0, 0)

        if a == 3:
            multiply(0, 4 * plain)
            copies["cs", a].wait_recv()
            multiply(4 * plain, 4 * width)
        else:
            copies["cs", a].wait_recv()
            multiply(0, 4 * width)

        live = rows_ref[0] - tile * local_rows
        step = 8 * TOPK

        def lanes(g, carry):
            def ordered(j):
                base = pl.multiple_of(j * step, step)
                ids = lax.broadcasted_iota(jnp.int32, (8, q), 0) + base
                values = []
                for i in range(TOPK):
                    value = acc[g, pl.ds(base + 8 * i, 8), :]
                    values.append(jnp.where(ids + 8 * i < live, value, lowest_score))
                return sort_down(values)

            def keep(values):
                for i in range(TOPK):
                    best[i] = values[i]

            def block(j, carry):
                keep(merge_top([best[i] for i in range(TOPK)], ordered(j)))
                return carry

            keep(ordered(0))
            lax.fori_loop(1, local_rows // step, block, 0)
            merged = over_sublanes([best[i] for i in range(TOPK)])
            for i in range(TOPK):
                sent[a, g, i:i + 1, :] = merged[i][0:1]
            return carry

        lax.fori_loop(0, 2, lanes, 0)
        for yr in range(2):
            if a or yr:
                n = len(copies) + 10
                copies["h", a, yr] = copy_to(
                    n, 60 + me, sent.at[a, yr], homed.at[pl.ds(me * TOPK, TOPK)], home(a, yr)
                )
                copies["h", a, yr].start()
            else:
                homed[pl.ds(pl.multiple_of(me * TOPK, TOPK), TOPK)] = sent[0, 0]

    plane_first()
    units[0].start()

    @pl.when(inner)
    def _():
        units[1].start()

    plane_second()
    first(0)
    plane_third()
    planes[0].start()

    @pl.when(inner)
    def _():
        planes[1].start()

    plane_over(0)
    arrived(1)

    @pl.when(inner)
    def _():
        units[2].start()
        arrived(2)
        units[3].start()

    first(1)
    second(0)

    @pl.when(inner)
    def _():
        arrived(3)
        units[4].start()

    plane_arrived(1)
    plane_over(1)

    @pl.when(inner)
    def _():
        planes[2].start()
        plane_arrived(2)
        planes[3].start()

    @pl.when(outer)
    def _():
        arrived(2)

    first(2)
    third(0)
    for load in loads[2:]:
        load.wait()
    compute(0)
    second(1)

    @pl.when(inner)
    def _():
        plane_arrived(3)
        planes[4].start()

    @pl.when(outer)
    def _():
        arrived(3)

    first(3)
    third(1)
    compute(1)
    second(2)

    @pl.when(outer)
    def _():
        plane_arrived(2)

    plane_over(2)
    second(3)
    third(2)
    compute(2)

    @pl.when(outer)
    def _():
        plane_arrived(3)

    plane_over(3)
    third(3)
    compute(3)

    for d in range(1, 8):
        source = (me + d) % 8
        copy_to(
            0, 60 + source, sent.at[0, 0], homed.at[pl.ds(source * TOPK, TOPK)], home(0, 1)
        ).wait_recv()
    shard = lax.broadcasted_iota(jnp.int32, (8, q), 0)
    named = shard == cand[0:1, :]
    for c in range(1, cand.shape[0]):
        named = named | (shard == cand[c:c + 1, :])
    merged = over_sublanes([
        jnp.where(named, homed[pl.ds(i, 8, stride=TOPK), :], lowest_score) for i in range(TOPK)
    ])
    for i in range(TOPK):
        tiles[i:i + 1, :] = merged[i][0:1]
    for t in range(1, 4):
        send(("t", t), tiles.at[pl.ds(0, TOPK)], tiles.at[pl.ds(t * TOPK, TOPK)], at(t))
    for t in range(1, 4):
        copies["t", t].wait_recv()
    merged = over_sublanes([tiles[pl.ds(i, 8, stride=TOPK), :] for i in range(TOPK)])
    for i in range(TOPK):
        out_ref[i:i + 1, :] = merged[i][0:1]
    for copy in copies.values():
        copy.wait_send()
    units[0].wait_send()
    planes[0].wait_send()

    @pl.when(inner)
    def _():
        for copy in units[1:] + planes[1:]:
            copy.wait_send()


def fused(test_grads, fisher, train_grads, candidates, shard_rows):
    q, width = test_grads.shape
    local_rows, columns = train_grads.shape
    far = pl.BlockSpec(memory_space=pl.ANY)
    best = pl.pallas_call(
        kernel,
        out_shape=jax.ShapeDtypeStruct((TOPK, q), jnp.float32),
        in_specs=[far] * 4 + [pl.BlockSpec(memory_space=pltpu.SMEM)],
        out_specs=pl.BlockSpec(memory_space=pltpu.VMEM),
        scratch_shapes=[
            pltpu.VMEM(test_grads.shape, jnp.bfloat16),
            pltpu.VMEM(fisher.shape, jnp.bfloat16),
            pltpu.VMEM((local_rows, columns), jnp.bfloat16),
            pltpu.VMEM(candidates.shape[::-1], jnp.int32),
            pltpu.VMEM((4, 2, columns, q), jnp.bfloat16),
            pltpu.VMEM((2, local_rows, q), jnp.float32),
            pltpu.VMEM((TOPK, 8, q), jnp.float32),
            pltpu.VMEM((4, 2, TOPK, q), jnp.float32),
            pltpu.VMEM((8 * TOPK, q), jnp.float32),
            pltpu.VMEM((8 * TOPK, q), jnp.float32),
            pltpu.SemaphoreType.DMA((68,)),
            pltpu.SemaphoreType.DMA((68,)),
            pltpu.SemaphoreType.DMA((11,)),
        ],
        compiler_params=pltpu.CompilerParams(
            collective_id=0, has_side_effects=True, vmem_limit_bytes=56 * 1024 * 1024
        ),
    )(test_grads, fisher, train_grads, candidates.T, shard_rows)
    return best.T


def solution(mesh):
    placed = (
        P("train", "tile"),
        P("tile", None, None),
        P(("train", "tile"), None),
        P("train", None),
        P("train"),
    )
    sizes = (mesh.shape["train"], mesh.shape["tile"])
    return jax.shard_map(
        fused if sizes == (8, 4) else shards,
        mesh=mesh, in_specs=placed, out_specs=P("train", None), check_vma=False,
    )
```
